128 devices in a mesh: slit: 16 (over x, y_hi, core), span: 8 (over z, y_lo).
Axes of the slice: x: 4, y: 4 (y_hi: 2, y_lo: 2; y = y_hi * 2 + y_lo), z: 4, core: 2. Of those that a mesh axis runs over, the one named last changes fastest.
Arguments:
- query_tiles: bfloat16 [64, 16, 128, 768], P('slit', 'span'), may hold values from -4 to 4
- key_tiles: bfloat16 [64, 16, 128, 768], P('slit', 'span'), may hold values from -4 to 4
- value_tiles: bfloat16 [64, 16, 128, 768], P('slit', 'span'), may hold values from -3 to 3
- forward_out: bfloat16 [64, 16, 128, 768], P('slit', 'span'), may hold values from -3 to 3
- out_grad: bfloat16 [64, 16, 128, 768], P('slit', 'span'), may hold values from -3 to 3
- row_lse: float32 [64, 16, 12, 128], P('slit', 'span'), may hold values from 2 to 3.5
- neighbours: int32 [64, 16, 8], P('slit', 'span'), may hold values from 0 to 1023, as said below
- flags: int32 [64, 16, 8], P('slit', 'span'), may hold values from 0 to 1
Outputs:
- query_grad: bfloat16 [64, 16, 128, 768], P('slit', 'span')
- key_grad: bfloat16 [64, 16, 128, 768], P('slit', 'span')
- value_grad: bfloat16 [64, 16, 128, 768], P('slit', 'span')
The draws below stay inside these ranges and needn't reach their ends.
Inputs may be any that keep to these rules, and one draw needn't show every extreme that they name: `neighbours`: every listed key block lies within one block of its query block along both directions (slit positions taken modulo 64, transverse positions not wrapped); the entries with flag 1 come first in each list, are distinct, number at least 1, and some query block has all 8 entries used; padded entries hold the query block's own id.
All inputs are finite; a program needn't handle non-finite values.
Results may differ from the reference program's by a relative error of at most 0.006.
Values may be sent and summed in bfloat16 or wider, within the bound.
No kernel may reach another device: no remote copies, remote signals or barrier semaphores. Data moves between devices by JAX's collectives and lax.ppermute only.
A program may use at most 192 MiB of HBM per device.

```python
import math
import jax
import jax.numpy as jnp
import numpy as np
from jax import lax

D = 768
H = 12
HD = 64
BLK = 128
KMAX = 8
NA = 64
NB = 16


def neighbour_lists(key):
    first_key, second_key, third_key = jax.random.split(key, 3)
    off_slit = jnp.asarray(np.array([-1, -1, -1, 0, 0, 0, 1, 1, 1], np.int32))
    off_span = jnp.asarray(np.array([-1, 0, 1, -1, 0, 1, -1, 0, 1], np.int32))
    grid_a = jnp.broadcast_to(jnp.arange(NA, dtype=jnp.int32)[:, None], (NA, NB))
    grid_b = jnp.broadcast_to(jnp.arange(NB, dtype=jnp.int32)[None, :], (NA, NB))
    span_to = grid_b[:, :, None] + off_span[None, None, :]
    inside = (span_to >= 0) & (span_to < NB)
    ranking = jax.random.randint(first_key, (NA, NB, 9), 0, 1024) * 16 + jnp.arange(9, dtype=jnp.int32)
    ranking = jnp.where(inside, ranking, 1 << 20)
    order = jnp.argsort(ranking, axis=-1, stable=True)[:, :, :KMAX].astype(jnp.int32)
    count_in = jnp.sum(inside.astype(jnp.int32), axis=-1)
    centre = jax.random.randint(second_key, (), 0, NA)
    band_width = max(1, NA // 8)
    in_band = (grid_a - centre) % NA < band_width
    light = jax.random.randint(third_key, (NA, NB), 1, 4)
    counts = jnp.minimum(jnp.where(in_band, KMAX, light), count_in)
    position = jnp.arange(KMAX, dtype=jnp.int32)
    used = position[None, None, :] < counts[:, :, None]
    target_a = (grid_a[:, :, None] + off_slit[order]) % NA
    target_b = grid_b[:, :, None] + off_span[order]
    own_id = (grid_a * NB + grid_b)[:, :, None]
    ids = jnp.where(used, target_a * NB + target_b, own_id)
    return (ids.astype(jnp.int32), used.astype(jnp.int32))


def draw_neighbours(key, part):
    shared = neighbour_lists(key)
    return shared[0]


def draw_flags(key, part):
    shared = neighbour_lists(key)
    return shared[1]


def block_levels(key, dims, cuts, low, top_value):
    def one(dim, parts):
        heights = jax.random.uniform(jax.random.fold_in(jax.random.fold_in(key, 6), dim), (parts,), jnp.float32, low / len(cuts), top_value / len(cuts))
        return jnp.repeat(jnp.exp(heights), dims[dim] // parts).reshape((-1,) + (1,) * (len(dims) - dim - 1))

    gain = one(*cuts[0])
    for cut in cuts[1:]:
        gain = gain * one(*cut)
    return gain


def gaussian(rng, dims, width, reach, cuts=(), held_as=jnp.bfloat16):
    level = block_levels(rng, dims, cuts, -0.22, 0.18) if cuts else 1.0
    drawn = jax.random.normal(rng, dims, jnp.float32) * width * level
    return jnp.minimum(jnp.maximum(drawn, -reach), reach).astype(held_as)


def setup_inputs(seed: int = 0) -> dict:
    streams_of = jax.random.split(jax.random.key(seed), 9)
    query_tiles = gaussian(streams_of[0], (NA, NB, BLK, D), 1.0, 4.0, ((0, 16), (1, 8)))
    key_tiles = gaussian(streams_of[1], (NA, NB, BLK, D), 1.0, 4.0, ((0, 16), (1, 8)))
    value_tiles = gaussian(streams_of[2], (NA, NB, BLK, D), 0.5, 3.0, ((0, 16), (1, 8)))
    forward_out = gaussian(streams_of[3], (NA, NB, BLK, D), 0.5, 3.0, ((0, 16), (1, 8)))
    out_grad = gaussian(streams_of[4], (NA, NB, BLK, D), 0.5, 3.0, ((0, 16), (1, 8)))
    row_lse = jnp.clip(2.0 + 1.5 * jax.random.uniform(streams_of[5], (NA, NB, H, BLK), jnp.float32) ** block_levels(streams_of[5], (NA, NB, H, BLK), ((0, 16), (1, 8)), -0.2, 0.2), 2.0, 3.5)
    neighbours = draw_neighbours(jax.random.fold_in(streams_of[8], 71), 0)
    flags = draw_flags(jax.random.fold_in(streams_of[8], 71), 0)
    return {"query_tiles": query_tiles, "key_tiles": key_tiles, "value_tiles": value_tiles, "forward_out": forward_out, "out_grad": out_grad, "row_lse": row_lse, "neighbours": neighbours, "flags": flags}


def reference(query_tiles, key_tiles, value_tiles, forward_out, out_grad, row_lse, neighbours, flags):
    factor = 1.0 / math.sqrt(HD)
    nblocks = NA * NB
    query_all = query_tiles.reshape(nblocks, BLK, H, HD)
    key_all = key_tiles.reshape(nblocks, BLK, H, HD)
    value_all = value_tiles.reshape(nblocks, BLK, H, HD)
    grad_all = out_grad.reshape(nblocks, BLK, H, HD)
    out_all = forward_out.reshape(nblocks, BLK, H, HD)
    delta = lax.optimization_barrier(jnp.sum(grad_all.astype(jnp.float32) * out_all.astype(jnp.float32), axis=-1))
    delta = jnp.transpose(delta, (0, 2, 1))
    lse_all = row_lse.reshape(nblocks, H, BLK)
    id_lists = neighbours.reshape(nblocks, KMAX).astype(jnp.int32)
    masks = flags.reshape(nblocks, KMAX).astype(jnp.float32)

    def advance(running, item):
        key_acc, value_acc = running
        query_blk, grad_blk, lse_blk, delta_blk, id_row, mask_row = item
        key_sel = key_all[id_row].astype(jnp.float32)
        value_sel = value_all[id_row].astype(jnp.float32)
        query_f = query_blk.astype(jnp.float32)
        grad_f = grad_blk.astype(jnp.float32)
        scores = jnp.einsum('thd,muhd->htmu', query_f, key_sel) * factor
        probs = jnp.exp(scores - lse_blk[:, :, None, None]) * mask_row[None, None, :, None]
        probs_low = lax.optimization_barrier(probs.astype(jnp.bfloat16)).astype(jnp.float32)
        value_part = jnp.einsum('htmu,thd->muhd', probs_low, grad_f)
        prob_grad = jnp.einsum('thd,muhd->htmu', grad_f, value_sel)
        score_grad = probs * (prob_grad - delta_blk[:, :, None, None])
        score_grad = lax.optimization_barrier(score_grad.astype(jnp.bfloat16)).astype(jnp.float32)
        query_part = jnp.einsum('htmu,muhd->thd', score_grad, key_sel) * factor
        key_part = jnp.einsum('htmu,thd->muhd', score_grad, query_f) * factor
        key_acc = key_acc.at[id_row].add(key_part)
        value_acc = value_acc.at[id_row].add(value_part)
        return ((key_acc, value_acc), query_part.astype(jnp.bfloat16))
    zeros_acc = jnp.zeros((nblocks, BLK, H, HD), jnp.float32)
    (key_acc, value_acc), query_parts = lax.scan(advance, (zeros_acc, zeros_acc), (query_all, grad_all, lse_all, delta, id_lists, masks))
    shape_out = (NA, NB, BLK, D)
    query_grad = query_parts.reshape(shape_out)
    key_grad = key_acc.reshape(shape_out).astype(jnp.bfloat16)
    value_grad = value_acc.reshape(shape_out).astype(jnp.bfloat16)
    return (query_grad, key_grad, value_grad)
```

```python
import functools

import jax
import jax.numpy as jnp
from jax import lax
from jax.experimental import pallas as pl
from jax.experimental.pallas import tpu as pltpu
from jax.sharding import PartitionSpec as P

CHUNKS = ((0, 2), (2, 2), (4, 2))
BLK = 128
PAIR = 128
HALF = 64
PAY = 2 * BLK + 16
FAR = 1.0e4
SCALE = 0.125
AXES = ("slit", "span")
VMEM = 56 * 1024 * 1024

NT = (((1,), (1,)), ((), ()))
NN = (((1,), (0,)), ((), ()))


def dot(a, b, dims):
    return lax.dot_general(a, b, dims, preferred_element_type=jnp.float32)


def head_masks():
    lane = lax.broadcasted_iota(jnp.int32, (1, PAIR), 1)
    first = jnp.where(lane < HALF, 1.0, 0.0)
    return first.astype(jnp.bfloat16), (1.0 - first).astype(jnp.bfloat16)


def split_heads(x, masks):
    return jnp.concatenate([x * masks[0], x * masks[1]], axis=0)


def offset_row(dr, dc):
    o = (dr + 1) * 3 + dc + 1
    return 8 if o == 4 else (o if o < 4 else o - 1)


def attend(keys, values, keys_t, queries, masks):
    probs_all, grads_all, q_all, do_all, dq_t = [], [], [], [], []
    for q, do, lse, delta, biases in queries:
        q2 = split_heads(q * jnp.asarray(SCALE, jnp.bfloat16), masks)
        do2 = split_heads(do, masks)
        s = dot(keys, q2, NT)
        dp = dot(values, do2, NT)
        p_parts, g_parts = [], []
        for n, bias in enumerate(biases):
            part = slice(n * BLK, (n + 1) * BLK)
            p = jnp.exp(s[part] - (lse + bias))
            p_parts.append(p.astype(jnp.bfloat16))
            g_parts.append((p * (dp[part] - delta)).astype(jnp.bfloat16))
        p = jnp.concatenate(p_parts, axis=0) if len(p_parts) > 1 else p_parts[0]
        g = jnp.concatenate(g_parts, axis=0) if len(g_parts) > 1 else g_parts[0]
        dq_t.append(
            (dot(keys_t[:HALF], g[:, :BLK], NN), dot(keys_t[HALF:], g[:, BLK:], NN))
        )
        probs_all.append(p)
        grads_all.append(g)
        q_all.append(q2)
        do_all.append(do2)
    cat = lambda xs, axis: jnp.concatenate(xs, axis=axis) if len(xs) > 1 else xs[0]
    dv = dot(cat(probs_all, 1), cat(do_all, 0), NN)
    dk = dot(cat(grads_all, 1), cat(q_all, 0), NN)
    return dk, dv, dq_t


def transpose_keys(k_ref, kt_ref):
    for r in range(4):
        for c in range(2):
            kt_ref[r, :, c * BLK : (c + 1) * BLK] = (
                k_ref[r, c].astype(jnp.float32).T.astype(jnp.bfloat16)
            )


def add_t(ref, index, parts):
    ref[index + (slice(0, HALF),)] += parts[0]
    ref[index + (slice(HALF, PAIR),)] += parts[1]


def prep_kernel(par_ref, q_ref, do_ref, o_ref, lse_ref, used_ref, col0_ref, col1_ref, out_ref, in_ref, dg0_ref, dg1_ref, delta_ref, aux_ref):
    outer = 3 * par_ref[0]
    inner = 3 - outer
    prod = do_ref[...].astype(jnp.float32) * o_ref[...].astype(jnp.float32)
    prod = prod.reshape(8 * BLK, PAIR)
    high = prod.astype(jnp.bfloat16)
    low = (prod - high.astype(jnp.float32)).astype(jnp.bfloat16)
    row = lax.broadcasted_iota(jnp.int32, (16, PAIR), 0)
    lane = lax.broadcasted_iota(jnp.int32, (16, PAIR), 1)
    pick = jnp.where(row == lane // HALF, 1.0, 0.0).astype(jnp.bfloat16)
    delta = dot(pick, high, NT) + dot(pick, low, NT)
    for r in range(4):
        for c in range(2):
            b = 2 * r + c
            d = delta[0:2, b * BLK : (b + 1) * BLK]
            delta_ref[r, c, 0] = d
            for at, x in ((0, lse_ref[r, c, 0]), (4, d)):
                x_high = x.astype(jnp.bfloat16).astype(jnp.float32)
                aux_ref[r, c, at : at + 2] = x_high
                aux_ref[r, c, at + 2 : at + 4] = x - x_high
            aux_ref[r, c, 8:16] = used_ref[r, c, 0:8]

    def pack(dst, at, r, c):
        dst[at, 0:BLK] = q_ref[r, c]
        dst[at, BLK : 2 * BLK] = do_ref[r, c]
        dst[at, 2 * BLK : PAY] = aux_ref[r, c].astype(jnp.bfloat16)

    for r in range(4):
        pack(col0_ref, r, r, 0)
        pack(col1_ref, r, r, 1)
    for c in range(2):
        pack(out_ref, c, outer, c)
        pack(in_ref, c, inner, c)
    pack(dg0_ref, 0, outer, 0)
    pack(dg1_ref, 0, outer, 1)


def local_kernel(q_ref, do_ref, k_ref, v_ref, lse_ref, delta_ref, used_ref, dk_ref, dv_ref, dq_ref, kt_ref, acc_ref):
    masks = head_masks()
    transpose_keys(k_ref, kt_ref)
    acc_ref[...] = jnp.zeros_like(acc_ref)
    dk_ref[...] = jnp.zeros_like(dk_ref)
    dv_ref[...] = jnp.zeros_like(dv_ref)

    def step(n, carry):
        r = (n + 1) // 3
        shift = (n + 1) % 3
        rq = r - 1 + shift
        keys = k_ref[r].reshape(2 * BLK, PAIR)
        values = v_ref[r].reshape(2 * BLK, PAIR)
        queries = []
        for c in range(2):
            lse = lse_ref[rq, c, 0]
            delta = delta_ref[rq, c, 0]
            biases = []
            for kc in range(2):
                o = (2 - shift) * 3 + kc - c + 1
                o = jnp.where(o == 4, 8, jnp.where(o > 4, o - 1, o))
                used = used_ref[rq, c, pl.ds(o, 1), :]
                bias = (1.0 - used) * FAR
                biases.append(jnp.concatenate([bias, bias], axis=1))
            queries.append(
                (
                    q_ref[rq, c],
                    do_ref[rq, c],
                    jnp.concatenate([lse[0:1], lse[1:2]], axis=1),
                    jnp.concatenate([delta[0:1], delta[1:2]], axis=1),
                    biases,
                )
            )
        dk, dv, dq_t = attend(keys, values, kt_ref[r], queries, masks)
        dk_ref[r] += dk.reshape(2, BLK, PAIR)
        dv_ref[r] += dv.reshape(2, BLK, PAIR)
        for c in range(2):
            add_t(acc_ref, (rq, c), dq_t[c])
        return carry

    lax.fori_loop(0, 10, step, 0)
    for r in range(4):
        for c in range(2):
            dq_ref[r, c] = acc_ref[r, c].T * SCALE


def remote_kernel(par_ref, k_ref, v_ref, col0_ref, col1_ref, out_ref, in_ref, dg0_ref, dg1_ref, dkp_ref, dvp_ref, *rest):
    dk_ref, dv_ref, r0_ref, r1_ref, ro_ref, ri_ref, rg0_ref, rg1_ref, kt_ref, acck_ref, accv_ref, accq_ref, aux_ref = rest[-13:]
    masks = head_masks()
    par = par_ref[0]
    outer = 3 * par
    inner = 3 - outer
    transpose_keys(k_ref, kt_ref)
    acck_ref[...] = dkp_ref[...]
    accv_ref[...] = dvp_ref[...]
    slots = (
        [(col0_ref, i) for i in range(4)]
        + [(col1_ref, i) for i in range(4)]
        + [(out_ref, 0), (out_ref, 1)]
        + [(in_ref, i) for i in range(4)]
        + [(dg0_ref, 0), (dg1_ref, 0)]
    )
    for i, (ref, at) in enumerate(slots):
        aux_ref[i] = ref[at, 2 * BLK : PAY].astype(jnp.float32)

    def query(i, rows):
        ref, at = slots[i]
        stats = aux_ref[i, 0:8]
        lse = stats[0:2] + stats[2:4]
        delta = stats[4:6] + stats[6:8]
        biases = []
        for row in rows:
            bias = (1.0 - aux_ref[i, pl.ds(8 + row, 1), :]) * FAR
            biases.append(jnp.concatenate([bias, bias], axis=1))
        return (
            ref[at, 0:BLK],
            ref[at, BLK : 2 * BLK],
            jnp.concatenate([lse[0:1], lse[1:2]], axis=1),
            jnp.concatenate([delta[0:1], delta[1:2]], axis=1),
            biases,
        )

    def put(i, parts):
        accq_ref[i, 0:HALF] = parts[0]
        accq_ref[i, HALF:PAIR] = parts[1]

    for side in range(2):
        dc = 1 - 2 * side
        lanes = slice(side * BLK, (side + 1) * BLK)
        for a in (0, 2):
            keys = jnp.concatenate([k_ref[a, side], k_ref[a + 1, side]], axis=0)
            values = jnp.concatenate([v_ref[a, side], v_ref[a + 1, side]], axis=0)
            keys_t = jnp.concatenate([kt_ref[a, :, lanes], kt_ref[a + 1, :, lanes]], axis=1)
            queries = [
                query(4 * side + a, [offset_row(0, dc), offset_row(1, dc)]),
                query(4 * side + a + 1, [offset_row(-1, dc), offset_row(0, dc)]),
            ]
            dk, dv, dq_t = attend(keys, values, keys_t, queries, masks)
            for n in range(2):
                part = slice(n * BLK, (n + 1) * BLK)
                acck_ref[a + n, side] += dk[part]
                accv_ref[a + n, side] += dv[part]
                put(4 * side + a + n, dq_t[n])
    up, down = 0, 5
    row_outer = jnp.where(par == 0, down, up)
    row_inner = down + up - row_outer
    for side in range(2):
        dc = 1 - 2 * side
        lanes = slice(side * BLK, (side + 1) * BLK)
        singles = [
            (1, 4 * side + 2, offset_row(-1, dc), True),
            (2, 4 * side + 1, offset_row(1, dc), True),
            (outer, 14 + side, row_outer + dc + 1, False),
            (inner, 12 + side, row_inner + dc + 1, False),
        ]
        for r, i, row, more in singles:
            dk, dv, dq_t = attend(
                k_ref[r, side], v_ref[r, side], kt_ref[r, :, lanes], [query(i, [row])], masks
            )
            acck_ref[r, side] += dk
            accv_ref[r, side] += dv
            if more:
                add_t(accq_ref, (i,), dq_t[0])
            else:
                put(i, dq_t[0])
    for r, first, row in ((outer, 8, row_outer), (inner, 10, row_inner)):
        queries = [query(first + c, [row + kc - c + 1 for kc in range(2)]) for c in range(2)]
        dk, dv, dq_t = attend(
            k_ref[r].reshape(2 * BLK, PAIR), v_ref[r].reshape(2 * BLK, PAIR), kt_ref[r], queries, masks
        )
        acck_ref[r] += dk.reshape(2, BLK, PAIR)
        accv_ref[r] += dv.reshape(2, BLK, PAIR)
        for c in range(2):
            put(first + c, dq_t[c])
    dk_ref[...] = acck_ref[...].astype(jnp.bfloat16)
    dv_ref[...] = accv_ref[...].astype(jnp.bfloat16)
    targets = (
        [(r0_ref, i) for i in range(4)]
        + [(r1_ref, i) for i in range(4)]
        + [(ro_ref, 0), (ro_ref, 1)]
        + [(ri_ref, i) for i in range(4)]
        + [(rg0_ref, 0), (rg1_ref, 0)]
    )
    for i, (ref, at) in enumerate(targets):
        ref[at] = (accq_ref[i].T * SCALE).astype(jnp.bfloat16)


def finish_kernel(par_ref, dq_ref, b0_ref, b1_ref, bo_ref, bi_ref, bg0_ref, bg1_ref, *rest):
    res_ref, acc_ref = rest[-2:]
    outer = 3 * par_ref[0]
    inner = 3 - outer
    f32 = jnp.float32
    for r in range(4):
        acc_ref[r, 0] = dq_ref[r, 0] + b0_ref[r].astype(f32)
        acc_ref[r, 1] = dq_ref[r, 1] + b1_ref[r].astype(f32)
    for c in range(2):
        acc_ref[outer, c] += bo_ref[c].astype(f32)
        acc_ref[inner, c] += bi_ref[c].astype(f32)
    acc_ref[outer, 0] += bg0_ref[0].astype(f32)
    acc_ref[outer, 1] += bg1_ref[0].astype(f32)
    res_ref[...] = acc_ref[...].astype(jnp.bfloat16)


def spec(shape, base=0):
    zeros = (0,) * (len(shape) - 1)
    return pl.BlockSpec(shape, lambda h: zeros + (h + base,))


def pair_spec(base=0):
    return pl.BlockSpec((4, 2, 1, 2, BLK), lambda h: (0, 0, h + base, 0, 0))


def used_spec():
    return pl.BlockSpec((4, 2, 16, BLK), lambda h: (0, 0, 0, 0))


SMEM = pl.BlockSpec(memory_space=pltpu.SMEM)
ANY = pl.BlockSpec(memory_space=pl.ANY)
TILES = (4, 2, BLK, PAIR)


def params():
    return pltpu.CompilerParams(vmem_limit_bytes=VMEM, dimension_semantics=("arbitrary",))


def cost(pairs, count):
    return pl.CostEstimate(
        flops=pairs * count * 2 * 5 * 2 * BLK * BLK * HALF * 4,
        bytes_accessed=pairs * count * 4 * BLK * PAIR * 2,
        transcendentals=pairs * count * 2 * BLK * BLK,
    )


def sds(shape, dtype=jnp.bfloat16):
    return jax.ShapeDtypeStruct(shape, dtype)


def prep(par, q, do, o, lse, used, base, count):
    width = count * PAIR
    shapes = [4, 4, 2, 2, 1, 1]
    return pl.pallas_call(
        prep_kernel,
        grid=(count,),
        in_specs=[SMEM] + [spec(TILES, base)] * 3 + [pair_spec(base), used_spec()],
        out_specs=[spec((n, PAY, PAIR)) for n in shapes] + [pair_spec()],
        out_shape=[sds((n, PAY, width)) for n in shapes] + [sds((4, 2, count, 2, BLK), jnp.float32)],
        scratch_shapes=[pltpu.VMEM((4, 2, 16, BLK), jnp.float32)],
        compiler_params=params(),
        name="prep",
    )(par, q, do, o, lse, used)


def local(q, do, k, v, lse, delta, used, base, count):
    width = count * PAIR
    full = sds((4, 2, BLK, width), jnp.float32)
    return pl.pallas_call(
        local_kernel,
        grid=(count,),
        in_specs=[spec(TILES, base)] * 4 + [pair_spec(base), pair_spec(), used_spec()],
        out_specs=[spec(TILES)] * 3,
        out_shape=[full] * 3,
        scratch_shapes=[
            pltpu.VMEM((4, PAIR, 2 * BLK), jnp.bfloat16),
            pltpu.VMEM(TILES, jnp.float32),
        ],
        compiler_params=params(),
        cost_estimate=cost(40, count),
        name="local",
    )(q, do, k, v, lse, delta, used)


def remote(par, k, v, halo, dkp, dvp, done, base, count):
    width = count * PAIR
    sizes = [4, 4, 2, 4, 1, 1]
    full = sds((4, 2, BLK, 6 * PAIR))
    return pl.pallas_call(
        remote_kernel,
        grid=(count,),
        in_specs=[SMEM]
        + [spec(TILES, base)] * 2
        + [spec((n, PAY, PAIR)) for n in sizes]
        + [spec(TILES)] * 2
        + [ANY] * len(done),
        out_specs=[spec(TILES, base)] * 2 + [spec((n, BLK, PAIR)) for n in sizes],
        out_shape=[full] * 2 + [sds((n, BLK, width)) for n in sizes],
        input_output_aliases={11 + i: i for i in range(len(done))},
        scratch_shapes=[
            pltpu.VMEM((4, PAIR, 2 * BLK), jnp.bfloat16),
            pltpu.VMEM(TILES, jnp.float32),
            pltpu.VMEM(TILES, jnp.float32),
            pltpu.VMEM((16, PAIR, BLK), jnp.float32),
            pltpu.VMEM((16, 16, BLK), jnp.float32),
        ],
        compiler_params=params(),
        cost_estimate=cost(32, count),
        name="remote",
    )(par, k, v, *halo, dkp, dvp, *done)


def finish(par, dqp, back, done, base, count):
    sizes = [4, 4, 2, 2, 1, 1]
    return pl.pallas_call(
        finish_kernel,
        grid=(count,),
        in_specs=[SMEM, spec(TILES)] + [spec((n, BLK, PAIR)) for n in sizes] + [ANY] * len(done),
        out_specs=spec(TILES, base),
        out_shape=sds((4, 2, BLK, 6 * PAIR)),
        input_output_aliases={8 + i: i for i in range(len(done))},
        scratch_shapes=[pltpu.VMEM(TILES, jnp.float32)],
        compiler_params=params(),
        name="finish",
    )(par, dqp, *back, *done)


def pairs_of(rows, cols):
    at = lambda s, p: (s % rows) * cols + p
    outer = lambda s: s + 1 if s % 2 else s - 1
    inner = lambda s: s - 1 if s % 2 else s + 1
    cells = [(s, p) for s in range(rows) for p in range(cols)]
    return {
        "right": [(at(s, p), at(s, p + 1)) for s, p in cells if p + 1 < cols],
        "left": [(at(s, p), at(s, p - 1)) for s, p in cells if p > 0],
        "outer": [(at(s, p), at(outer(s), p)) for s, p in cells],
        "inner": [(at(s, p), at(inner(s), p)) for s, p in cells],
        "outer_right": [(at(s, p), at(outer(s), p + 1)) for s, p in cells if p + 1 < cols],
        "outer_left": [(at(s, p), at(outer(s), p - 1)) for s, p in cells if p > 0],
    }


def list_masks(neighbours, flags, grid_a, grid_b):
    rows_a, rows_b = neighbours.shape[:2]
    a = lax.axis_index("slit") * rows_a + lax.broadcasted_iota(jnp.int32, (rows_a, rows_b, 16), 0)
    b = lax.axis_index("span") * rows_b + lax.broadcasted_iota(jnp.int32, (rows_a, rows_b, 16), 1)
    row = lax.broadcasted_iota(jnp.int32, (rows_a, rows_b, 16), 2)
    o = jnp.where(row == 8, 4, jnp.where(row < 4, row, row + 1))
    to_a = (a + o // 3 - 1 + grid_a) % grid_a
    to_b = b + o % 3 - 1
    valid = (row < 9) & (to_b >= 0) & (to_b < grid_b)
    ids = jnp.where(valid, to_a * grid_b + to_b, -1)
    hit = (neighbours[:, :, None, :] == ids[:, :, :, None]) & (flags[:, :, None, :] != 0)
    used = jnp.any(hit, axis=-1).astype(jnp.float32)
    return jnp.broadcast_to(used[:, :, :, None], (rows_a, rows_b, 16, BLK))


def on_device(rows, cols, q, k, v, o, do, lse, neighbours, flags):
    pairs = pairs_of(rows, cols)
    send = lambda x, way: lax.ppermute(x, AXES, pairs[way])
    par = lax.axis_index("slit") % 2
    pars = par.reshape(1).astype(jnp.int32)
    inner_row = 3 - 3 * par
    used = list_masks(neighbours, flags, 4 * rows, 2 * cols)
    lse = lse.reshape(4, 2, 6, 2, BLK)

    dks, dqs = (), ()
    for base, count in CHUNKS:
        col0, col1, out, inn, dg0, dg1, delta = prep(pars, q, do, o, lse, used, base, count)
        from_left = send(col1, "right")
        from_right = send(col0, "left")
        halo_out = send(out, "outer")
        halo_g0 = send(dg1, "outer_right")
        halo_g1 = send(dg0, "outer_left")
        dkp, dvp, dqp = local(q, do, k, v, lse, delta, used, base, count)
        corner0 = lax.dynamic_slice_in_dim(from_left, inner_row, 1, 0)
        corner1 = lax.dynamic_slice_in_dim(from_right, inner_row, 1, 0)
        halo_in = send(jnp.concatenate([inn, corner0, corner1], axis=0), "inner")
        halo = (from_left, from_right, halo_out, halo_in, halo_g0, halo_g1)
        dk, dv, r0, r1, ro, ri, rg0, rg1 = remote(pars, k, v, halo, dkp, dvp, dks, base, count)
        dks = (dk, dv)
        back_in = send(ri, "inner")
        index = (inner_row, 0, 0)
        r0 = lax.dynamic_update_slice(
            r0, lax.dynamic_slice_in_dim(r0, inner_row, 1, 0) + back_in[2:3], index
        )
        r1 = lax.dynamic_update_slice(
            r1, lax.dynamic_slice_in_dim(r1, inner_row, 1, 0) + back_in[3:4], index
        )
        back1 = send(r0, "left")
        back0 = send(r1, "right")
        back_out = send(ro, "outer")
        back_g1 = send(rg0, "outer_left")
        back_g0 = send(rg1, "outer_right")
        back = (back0, back1, back_out, back_in[0:2], back_g0, back_g1)
        dqs = (finish(pars, dqp, back, dqs, base, count),)
    return dqs[0], dks[0], dks[1]


def solution(mesh):
    tile = P("slit", "span", None, None)
    row = P("slit", "span", None)
    body = functools.partial(on_device, mesh.shape["slit"], mesh.shape["span"])
    return jax.shard_map(
        body,
        mesh=mesh,
        in_specs=(tile,) * 6 + (row,) * 2,
        out_specs=(tile,) * 3,
        check_vma=False,
    )
```

```python
import functools

import jax
import jax.numpy as jnp
from jax import lax
from jax.experimental import pallas as pl
from jax.experimental.pallas import tpu as pltpu
from jax.sharding import PartitionSpec as P

SUB = 2
BLK = 128
PAIR = 128
HALF = 64
PAIRS = 6
FIRST = 4
PAY = 2 * BLK + 16
FAR = 1.0e4
SCALE = 0.125
AXES = ("slit", "span")
VMEM = 64 * 1024 * 1024 - 128 * 1024
GRID_A = 64
GRID_B = 16

NT = (((1,), (1,)), ((), ()))
NN = (((1,), (0,)), ((), ()))


def dot(a, b, dims):
    return lax.dot_general(a, b, dims, preferred_element_type=jnp.float32)


def cat(xs, axis):
    return jnp.concatenate(xs, axis=axis) if len(xs) > 1 else xs[0]


def head_masks():
    lane = lax.broadcasted_iota(jnp.int32, (1, PAIR), 1)
    first = jnp.where(lane < HALF, 1.0, 0.0)
    return first.astype(jnp.bfloat16), (1.0 - first).astype(jnp.bfloat16)


def split_heads(x, masks):
    return jnp.concatenate([x * masks[0], x * masks[1]], axis=0)


def offset_row(dr, dc):
    o = (dr + 1) * 3 + dc + 1
    return 8 if o == 4 else (o if o < 4 else o - 1)


def twice(x):
    return jnp.concatenate([x, x], axis=1)


def attend(tasks, masks):
    scored = []
    for (q, do, _, _, _), keys, values, _ in tasks:
        q2 = split_heads(q * jnp.asarray(SCALE, jnp.bfloat16), masks)
        do2 = split_heads(do, masks)
        scored.append((q2, do2, dot(cat(keys, 0), q2, NT), dot(cat(values, 0), do2, NT)))
    weighted = []
    for ((_, _, lse, delta, biases), _, _, _), (_, _, s, dp) in zip(tasks, scored):
        p_parts, g_parts = [], []
        for n, bias in enumerate(biases):
            part = slice(n * BLK, (n + 1) * BLK)
            p = jnp.exp(s[part] - (lse + bias))
            p_parts.append(p.astype(jnp.bfloat16))
            g_parts.append((p * (dp[part] - delta)).astype(jnp.bfloat16))
        weighted.append((cat(p_parts, 0), cat(g_parts, 0)))
    results = []
    for (_, _, _, keys_t), (q2, do2, _, _), (p, g) in zip(tasks, scored, weighted):
        kt = cat(keys_t, 1)
        dv = dot(p, do2, NN)
        dk = dot(g, q2, NN)
        dq_t = jnp.concatenate(
            [dot(kt[:HALF], g[:, :BLK], NN), dot(kt[HALF:], g[:, BLK:], NN)], axis=0
        )
        results.append((dk, dv, dq_t))
    return results


def flip(block):
    return block.astype(jnp.float32).T.astype(jnp.bfloat16)


def by_rows(par, run, together=False):
    middle = [(1, [0, 1, 2]), (2, [1, 2, 3])]
    if not together:
        run(middle)

    for core, ends in enumerate(([(0, [0, 1]), (3, [2, 3, 4])], [(0, [-1, 0, 1]), (3, [2, 3])])):
        pl.when(par == core)(functools.partial(run, middle + ends if together else ends))


def row_sums(do, o):
    prod = do.astype(jnp.float32) * o.astype(jnp.float32)
    high = prod.astype(jnp.bfloat16)
    low = (prod - high.astype(jnp.float32)).astype(jnp.bfloat16)
    shape = (16, do.shape[1])
    row = lax.broadcasted_iota(jnp.int32, shape, 0)
    lane = lax.broadcasted_iota(jnp.int32, shape, 1)
    pick = jnp.where(row == lane // HALF, 1.0, 0.0).astype(jnp.bfloat16)
    return dot(pick, high, NT) + dot(pick, low, NT)


def mark_lists(pos_ref, near_ref, flag_ref, r, c, dst_ref, at):
    dst_ref[at] = jnp.zeros((16, BLK), jnp.float32)
    for e in range(8):
        key = near_ref[r, c, e]
        flag = flag_ref[r, c, e]
        da = key // GRID_B - (pos_ref[1] + r)
        da = jnp.where(da > 1, da - GRID_A, jnp.where(da < -1, da + GRID_A, da))
        db = key % GRID_B - (pos_ref[2] + c)
        o = (da + 1) * 3 + db + 1
        row = jnp.where(o == 4, 8, jnp.where(o > 4, o - 1, o))
        row = jnp.clip(jnp.where(flag != 0, row, 15), 0, 15)
        dst_ref[at + (pl.ds(row, 1),)] = jnp.ones((1, BLK), jnp.float32)


def fill_aux(aux_ref, lse, delta, used):
    for n in range(PAIRS):
        lanes = slice(n * BLK, (n + 1) * BLK)
        heads = slice(2 * n, 2 * n + 2)
        for start, x in ((0, lse[heads]), (4, delta[heads])):
            high = x.astype(jnp.bfloat16).astype(jnp.float32)
            aux_ref[start : start + 2, lanes] = high
            aux_ref[start + 2 : start + 4, lanes] = x - high
        aux_ref[8:16, lanes] = used


def prepare_column_kernel(pos_ref, near_ref, flag_ref, q_ref, do_ref, o_ref, lse_ref, col_ref, delta_ref, used_ref, aux_ref, *, c):
    delta = row_sums(do_ref[0, 0], o_ref[0, 0])[0 : 2 * PAIRS]
    mark_lists(pos_ref, near_ref, flag_ref, pl.program_id(0), c, used_ref, (0,))
    fill_aux(aux_ref, lse_ref[0, c], delta, used_ref[0, 0:8])
    delta_ref[0] = delta
    col_ref[0, 0:BLK] = q_ref[0, 0]
    col_ref[0, BLK : 2 * BLK] = do_ref[0, 0]
    col_ref[0, 2 * BLK : PAY] = aux_ref[...].astype(jnp.bfloat16)


def prepare_row_kernel(pos_ref, near_ref, flag_ref, q_ref, do_ref, o_ref, lse_ref, out_ref, dg0_ref, dg1_ref, used_ref, aux_ref):
    delta = row_sums(do_ref[...].reshape(2 * BLK, FULL), o_ref[...].reshape(2 * BLK, FULL))
    for c, dg_ref in ((0, dg0_ref), (1, dg1_ref)):
        mark_lists(pos_ref, near_ref, flag_ref, 3 * pos_ref[0], c, used_ref, (c,))
        fill_aux(aux_ref.at[c], lse_ref[0, c], delta[0 : 2 * PAIRS, c * BLK : (c + 1) * BLK], used_ref[c, 0:8])
        for dst, at in ((out_ref, c), (dg_ref, 0)):
            dst[at, 0:BLK] = q_ref[0, c]
            dst[at, BLK : 2 * BLK] = do_ref[0, c]
            dst[at, 2 * BLK : PAY] = aux_ref[c].astype(jnp.bfloat16)


def local_kernel(pos_ref, q_ref, do_ref, k_ref, v_ref, ks_ref, lse_ref, delta0_ref, delta1_ref, used0_ref, used1_ref, dk_ref, dv_ref, sk_ref, sv_ref, dq_ref, kt_ref):
    h = pl.program_id(0)
    masks = head_masks()
    for c in range(2):
        lanes = slice(c * BLK, (c + 1) * BLK)
        for r in range(4):
            kt_ref[r, :, lanes] = flip(k_ref[r, c])
        kt_ref[4, :, lanes] = flip(ks_ref[0, c])
    for ref in (dk_ref, dv_ref, sk_ref, sv_ref):
        ref[...] = jnp.zeros_like(ref)

    def one(row, key_rows):
        tasks = []
        for c, delta_ref, used_ref in ((0, delta0_ref, used0_ref), (1, delta1_ref, used1_ref)):
            lse = [lse_ref[row, c, pl.ds(2 * h + i, 1), :] for i in range(2)]
            delta = [delta_ref[row, pl.ds(2 * h + i, 1), :] for i in range(2)]
            keys, values, keys_t, biases = [], [], [], []
            for r in key_rows:
                for kc in range(2):
                    sibling = r in (-1, 4)
                    keys.append(ks_ref[0, kc] if sibling else k_ref[r, kc])
                    values.append(ks_ref[1, kc] if sibling else v_ref[r, kc])
                    keys_t.append(kt_ref[4 if sibling else r, :, kc * BLK : (kc + 1) * BLK])
                    at = offset_row(r - row, kc - c)
                    biases.append(twice((1.0 - used_ref[row, at : at + 1, :]) * FAR))
            query = (q_ref[row, c], do_ref[row, c], cat(lse, 1), cat(delta, 1), biases)
            tasks.append((query, keys, values, keys_t))
        results = attend(tasks, masks)
        dk = results[0][0] + results[1][0]
        dv = results[0][1] + results[1][1]
        for n, r in enumerate(key_rows):
            for kc in range(2):
                part = slice((2 * n + kc) * BLK, (2 * n + kc + 1) * BLK)
                if r in (-1, 4):
                    sk_ref[kc] += dk[part]
                    sv_ref[kc] += dv[part]
                else:
                    dk_ref[r, kc] += dk[part]
                    dv_ref[r, kc] += dv[part]
        for c in range(2):
            dq_ref[row, c] = results[c][2].T * SCALE

    def run(groups):
        for row, key_rows in groups:
            one(row, key_rows)

    by_rows(pos_ref[0], run)


def received(ref, at, lanes, aux, rows):
    lse = aux[0:2] + aux[2:4]
    delta = aux[4:6] + aux[6:8]
    biases = [twice((1.0 - row) * FAR) for row in rows]
    stats = [cat([x[0:1], x[1:2]], 1) for x in (lse, delta)]
    return (ref[at, 0:BLK, lanes], ref[at, BLK : 2 * BLK, lanes], stats[0], stats[1], biases)


def column_kernel(pos_ref, k_ref, v_ref, ks_ref, col_ref, dkp_ref, dvp_ref, skp_ref, svp_ref, *rest, side):
    dk_ref, dv_ref, sib_ref, tail_ref, res_ref, kt_ref, acck_ref, accv_ref, accs_ref = rest[-9:]
    masks = head_masks()
    for n in range(SUB):
        lanes = slice(n * PAIR, (n + 1) * PAIR)
        for r in range(4):
            kt_ref[n, :, r * BLK : (r + 1) * BLK] = flip(k_ref[r, 0, :, lanes])
        kt_ref[n, :, 4 * BLK :] = flip(ks_ref[0, 0, :, lanes])
    acck_ref[...] = dkp_ref[:, 0]
    accv_ref[...] = dvp_ref[:, 0]
    accs_ref[0] = skp_ref[0]
    accs_ref[1] = svp_ref[0]

    def run(groups):
        tasks, places = [], []
        for n in range(SUB):
            lanes = slice(n * PAIR, (n + 1) * PAIR)
            for row, key_rows in groups:
                aux = col_ref[row, 2 * BLK : PAY, lanes].astype(jnp.float32)
                keys, values, keys_t, rows = [], [], [], []
                for r in key_rows:
                    sibling = r in (-1, 4)
                    keys.append(ks_ref[0, 0, :, lanes] if sibling else k_ref[r, 0, :, lanes])
                    values.append(ks_ref[1, 0, :, lanes] if sibling else v_ref[r, 0, :, lanes])
                    at = 4 * BLK if sibling else r * BLK
                    keys_t.append(kt_ref[n, :, at : at + BLK])
                    at = 8 + offset_row(r - row, 1 - 2 * side)
                    rows.append(aux[at : at + 1])
                tasks.append((received(col_ref, row, lanes, aux, rows), keys, values, keys_t))
                places.append((row, key_rows, lanes))
        for (row, key_rows, lanes), (dk, dv, dq_t) in zip(places, attend(tasks, masks)):
            for n, r in enumerate(key_rows):
                part = slice(n * BLK, (n + 1) * BLK)
                if r in (-1, 4):
                    accs_ref[0, :, lanes] += dk[part]
                    accs_ref[1, :, lanes] += dv[part]
                else:
                    acck_ref[r, :, lanes] += dk[part]
                    accv_ref[r, :, lanes] += dv[part]
            res_ref[row, :, lanes] = (dq_t.T * SCALE).astype(jnp.bfloat16)

    by_rows(pos_ref[0], run, together=True)
    for r in range(4):
        dk_ref[r, 0] = acck_ref[r].astype(jnp.bfloat16)
        dv_ref[r, 0] = accv_ref[r].astype(jnp.bfloat16)
    sib_ref[0] = accs_ref[...].astype(jnp.bfloat16)
    for i in range(2):
        tail_ref[i, 0, 0] = acck_ref[3 * i]
        tail_ref[i, 0, 1] = accv_ref[3 * i]


def outer_kernel(pos_ref, k_ref, v_ref, out_ref, dg0_ref, dg1_ref, part_ref, ro_ref, rg0_ref, rg1_ref):
    masks = head_masks()
    below = pos_ref[0] == 0
    slots = ((dg0_ref, 0, rg0_ref, -1), (out_ref, 0, ro_ref, 0), (out_ref, 1, ro_ref, 1), (dg1_ref, 0, rg1_ref, 2))
    tasks, places = [], []
    for n in range(SUB):
        lanes = slice(n * PAIR, (n + 1) * PAIR)
        kts = [flip(k_ref[0, c, :, lanes]) for c in range(2)]
        for ref, at, res_ref, c in slots:
            near = [kc for kc in range(2) if abs(kc - c) <= 1]
            aux = ref[at, 2 * BLK : PAY, lanes].astype(jnp.float32)
            ups = [8 + kc - c + 1 for kc in near]
            rows = [jnp.where(below, aux[u + 5 : u + 6], aux[u : u + 1]) for u in ups]
            query = received(ref, at, lanes, aux, rows)
            keys = [k_ref[0, kc, :, lanes] for kc in near]
            values = [v_ref[0, kc, :, lanes] for kc in near]
            tasks.append((query, keys, values, [kts[kc] for kc in near]))
            places.append((lanes, at, res_ref, near))
    totals = {}
    for (lanes, at, res_ref, near), (dk, dv, dq_t) in zip(places, attend(tasks, masks)):
        for n, kc in enumerate(near):
            for i, x in enumerate((dk, dv)):
                x = x[n * BLK : (n + 1) * BLK]
                key = (kc, i, lanes.start)
                totals[key] = totals[key] + x if key in totals else x
        res_ref[at, :, lanes] = (dq_t.T * SCALE).astype(jnp.bfloat16)
    for (kc, i, start), x in totals.items():
        part_ref[kc, i, :, start : start + PAIR] = x


def queries_kernel(pos_ref, dq_ref, back_ref, row_ref, corner_ref, *rest):
    res_ref = rest[-1]
    for r in range(2):
        total = dq_ref[r, 0] + back_ref[r].astype(jnp.float32)
        edge = row_ref[0].astype(jnp.float32) + corner_ref[0].astype(jnp.float32)
        outer = 2 * pl.program_id(0) + r == 3 * pos_ref[0]
        res_ref[r, 0] = jnp.where(outer, total + edge, total).astype(jnp.bfloat16)


def edges_kernel(pos_ref, tail_ref, part_ref, sib_ref, dk_in, dv_in, dk_ref, dv_ref):
    outer = pl.program_id(0) == pos_ref[0]
    for c in range(2):
        for i, ref in enumerate((dk_ref, dv_ref)):
            add = jnp.where(outer, part_ref[c, i], sib_ref[c, i].astype(jnp.float32))
            ref[0, c] = (tail_ref[0, c, i] + add).astype(jnp.bfloat16)


def lanes_spec(shape, base=0, at=None):
    at = at or (0,) * (len(shape) - 1)
    return pl.BlockSpec(shape, lambda h, *_: at + (h + base,))


def rows_spec(shape, lane=0):
    return pl.BlockSpec(shape, lambda r, *_: (r,) + (0,) * (len(shape) - 2) + (lane,))


def fixed(shape, lane=0):
    return pl.BlockSpec(shape, lambda *_: (0,) * (len(shape) - 1) + (lane,))


SMEM = pl.BlockSpec(memory_space=pltpu.SMEM)
ANY = pl.BlockSpec(memory_space=pl.ANY)
TILES = (4, 2, BLK, PAIR)
FULL = PAIRS * PAIR


def sds(shape, dtype=jnp.bfloat16):
    return jax.ShapeDtypeStruct(shape, dtype)


def f32s(shape):
    return sds(shape, jnp.float32)


def call(kernel, name, grid, ins, outs, shapes, scratch=(), alias=None):
    return pl.pallas_call(
        kernel,
        grid_spec=pltpu.PrefetchScalarGridSpec(
            num_scalar_prefetch=1, grid=(grid,), in_specs=ins, out_specs=outs, scratch_shapes=scratch
        ),
        out_shape=shapes,
        input_output_aliases=alias or {},
        compiler_params=pltpu.CompilerParams(
            vmem_limit_bytes=VMEM, dimension_semantics=("arbitrary",)
        ),
        cost_estimate=pl.CostEstimate(flops=1, bytes_accessed=1, transcendentals=0),
        name=name,
    )


def prepare_column(pos, lists, q, do, o, lse, c):
    block = pl.BlockSpec((1, 1, BLK, FULL), lambda r, _: (r, c, 0, 0))
    shapes = [(PAY, FULL), (2 * PAIRS, BLK), (16, BLK)]
    kinds = [jnp.bfloat16, jnp.float32, jnp.float32]
    return call(
        functools.partial(prepare_column_kernel, c=c),
        "prepare_column",
        4,
        [SMEM] * 2 + [block] * 3 + [rows_spec((1, 2, 2 * PAIRS, BLK))],
        [rows_spec((1,) + shape) for shape in shapes],
        [sds((4,) + shape, kind) for shape, kind in zip(shapes, kinds)],
        [pltpu.VMEM((16, FULL), jnp.float32)],
    )(pos, *lists, q, do, o, lse)


def prepare_row(pos, lists, q, do, o, lse):
    outer = lambda shape: pl.BlockSpec(shape, lambda _, p: (3 * p[0], 0, 0, 0))
    shapes = [(2, PAY, FULL), (1, PAY, FULL), (1, PAY, FULL)]
    return call(
        prepare_row_kernel,
        "prepare_row",
        1,
        [SMEM] * 2 + [outer((1, 2, BLK, FULL))] * 3 + [outer((1, 2, 2 * PAIRS, BLK))],
        [fixed(shape) for shape in shapes],
        [sds(shape) for shape in shapes],
        [pltpu.VMEM((2, 16, BLK), jnp.float32), pltpu.VMEM((2, 16, FULL), jnp.float32)],
    )(pos, *lists, q, do, o, lse)


def local(pos, q, do, k, v, ks, lse, deltas, used):
    tiles = f32s((4, 2, BLK, FULL))
    edge = f32s((2, BLK, FULL))
    return call(
        local_kernel,
        "local",
        PAIRS,
        [lanes_spec(TILES)] * 4
        + [lanes_spec((2, 2, BLK, PAIR)), fixed((4, 2, 2 * PAIRS, BLK))]
        + [fixed((4, 2 * PAIRS, BLK))] * 2
        + [fixed((4, 16, BLK))] * 2,
        [lanes_spec(TILES)] * 2 + [lanes_spec((2, BLK, PAIR))] * 2 + [lanes_spec(TILES)],
        [tiles, tiles, edge, edge, tiles],
        [pltpu.VMEM((5, PAIR, 2 * BLK), jnp.bfloat16)],
    )(pos, q, do, k, v, ks, lse, *deltas, *used)


def column(pos, k, v, ks, col, parts, done, base, count, side):
    wide = SUB * PAIR
    at = base // SUB
    column_of = lanes_spec((4, 1, BLK, wide), at, (0, side, 0))
    return call(
        functools.partial(column_kernel, side=side),
        "column",
        count // SUB,
        [column_of] * 2
        + [lanes_spec((2, 1, BLK, wide), at, (0, side, 0)), lanes_spec((4, PAY, wide), at)]
        + [column_of] * 2
        + [lanes_spec((1, BLK, wide), at, (side, 0))] * 2
        + [ANY] * len(done),
        [column_of] * 2
        + [
            lanes_spec((1, 2, BLK, wide), at, (side, 0, 0)),
            lanes_spec((2, 1, 2, BLK, wide), at, (0, side, 0, 0)),
            lanes_spec((4, BLK, wide)),
        ],
        [sds((4, 2, BLK, FULL))] * 2
        + [sds((2, 2, BLK, FULL)), f32s((2, 2, 2, BLK, FULL)), sds((4, BLK, count * PAIR))],
        [pltpu.VMEM((SUB, PAIR, 5 * BLK), jnp.bfloat16)]
        + [pltpu.VMEM((4, BLK, wide), jnp.float32)] * 2
        + [pltpu.VMEM((2, BLK, wide), jnp.float32)],
        alias={9 + i: i for i in range(len(done))},
    )(pos, k, v, ks, col, *parts, *done)


def outers(pos, k, v, out, dg0, dg1):
    sizes = (2, 1, 1)
    wide = SUB * PAIR
    outer = pl.BlockSpec((1, 2, BLK, wide), lambda h, p: (3 * p[0], 0, 0, h))
    return call(
        outer_kernel,
        "outer_rows",
        PAIRS // SUB,
        [outer] * 2 + [lanes_spec((n, PAY, wide)) for n in sizes],
        [lanes_spec((2, 2, BLK, wide))] + [lanes_spec((n, BLK, wide)) for n in sizes],
        [f32s((2, 2, BLK, FULL))] + [sds((n, BLK, FULL)) for n in sizes],
    )(pos, k, v, out, dg0, dg1)


def finish_queries(pos, dqp, back, back_out, corner, done, c, base, count):
    wide = count * PAIR
    lane = base // count
    block = pl.BlockSpec((2, 1, BLK, wide), lambda r, *_: (r, c, 0, lane))
    edge = lambda at: pl.BlockSpec((1, BLK, wide), lambda *_: (at, 0, lane))
    return call(
        queries_kernel,
        "finish_queries",
        2,
        [block, rows_spec((2, BLK, wide)), edge(c), edge(0)] + [ANY] * len(done),
        block,
        sds((4, 2, BLK, FULL)),
        alias={5 + i: i for i in range(len(done))},
    )(pos, dqp, back, back_out, corner, *done)


def finish_edges(pos, tail, part, sib, dk, dv):
    row = pl.BlockSpec((1, 2, BLK, FULL), lambda i, p: (3 * i, 0, 0, 0))
    edge = (2, 2, BLK, FULL)
    return call(
        edges_kernel,
        "finish_edges",
        2,
        [rows_spec((1,) + edge)] + [fixed(edge)] * 2 + [ANY] * 2,
        [row] * 2,
        [sds((4, 2, BLK, FULL))] * 2,
        alias={4: 0, 5: 1},
    )(pos, tail, part, sib, dk, dv)


def pairs_of(rows, cols):
    at = lambda s, p: (s % rows) * cols + p
    outer = lambda s: s + 1 if s % 2 else s - 1
    inner = lambda s: s - 1 if s % 2 else s + 1
    cells = [(s, p) for s in range(rows) for p in range(cols)]
    return {
        "right": [(at(s, p), at(s, p + 1)) for s, p in cells if p + 1 < cols],
        "left": [(at(s, p), at(s, p - 1)) for s, p in cells if p > 0],
        "outer": [(at(s, p), at(outer(s), p)) for s, p in cells],
        "inner": [(at(s, p), at(inner(s), p)) for s, p in cells],
        "outer_right": [(at(s, p), at(outer(s), p + 1)) for s, p in cells if p + 1 < cols],
        "outer_left": [(at(s, p), at(outer(s), p - 1)) for s, p in cells if p > 0],
    }


def after(pos, *others):
    return lax.optimization_barrier((pos,) + others)[0]


def on_device(rows, cols, q, k, v, o, do, lse, neighbours, flags):
    pairs = pairs_of(rows, cols)
    send = lambda x, way: lax.ppermute(x, AXES, pairs[way])
    row = lax.axis_index("slit")
    pos = jnp.stack([row % 2, row * 4, lax.axis_index("span") * 2]).astype(jnp.int32)
    lists = (neighbours, flags)

    out, dg0, dg1 = prepare_row(pos, lists, q, do, o, lse)
    halo_out = send(out, "outer")
    pos = after(pos, out)
    inner = 3 - 3 * (row % 2)
    kv = jnp.concatenate([lax.dynamic_slice_in_dim(x, inner, 1, 0) for x in (k, v)], axis=0)
    ks = send(kv, "inner")
    col1, delta1, used1 = prepare_column(pos, lists, q, do, o, lse, 1)
    pos = after(pos, delta1)
    col0, delta0, used0 = prepare_column(pos, lists, q, do, o, lse, 0)
    from_left = send(after(col1, halo_out, ks, delta0), "right")
    from_right = send(after(col0, halo_out, ks), "left")
    halo_g0 = send(dg1, "outer_right")
    halo_g1 = send(dg0, "outer_left")
    pos = after(pos, delta0)

    *parts, dqp = local(pos, q, do, k, v, ks, lse, (delta0, delta1), (used0, used1))
    pos = after(pos, dqp)
    *done, res0 = column(pos, k, v, ks, from_left, parts, (), 0, PAIRS, 0)
    back1 = send(res0, "left")
    pos = after(pos, res0)
    part_out, ro, rg0, rg1 = outers(pos, k, v, halo_out, halo_g0, halo_g1)
    back_out = send(ro, "outer")
    back_g1 = send(rg0, "outer_left")
    back_g0 = send(rg1, "outer_right")
    pos = after(pos, ro)
    *done, res1 = column(pos, k, v, ks, from_right, parts, done, 0, FIRST, 1)
    back0 = send(res1, "right")
    pos = after(pos, res1, back1, back_out, back_g0, back_g1)
    dk, dv, sib, tail, res2 = column(pos, k, v, ks, from_right, parts, done, FIRST, PAIRS - FIRST, 1)
    back0_last = send(res2, "right")

    dq = finish_queries(pos, dqp, back1, back_out, back_g1, (), 1, 0, PAIRS)
    back_sib = send(after(sib, dq), "inner")
    pos = after(pos, dq)
    dk, dv = finish_edges(pos, tail, part_out, back_sib, dk, dv)
    pos = after(pos, dk)
    dq = finish_queries(pos, dqp, back0, back_out, back_g0, (dq,), 0, 0, FIRST)
    dq = finish_queries(pos, dqp, back0_last, back_out, back_g0, (dq,), 0, FIRST, PAIRS - FIRST)
    return dq, dk, dv


def solution(mesh):
    tile = P("slit", "span", None, None)
    row = P("slit", "span", None)
    body = functools.partial(on_device, mesh.shape["slit"], mesh.shape["span"])
    return jax.shard_map(
        body,
        mesh=mesh,
        in_specs=(tile,) * 6 + (row,) * 2,
        out_specs=(tile,) * 3,
        check_vma=False,
    )
```

```python
import functools

import jax
import jax.numpy as jnp
from jax import lax
from jax.experimental import pallas as pl
from jax.experimental.pallas import tpu as pltpu
from jax.sharding import PartitionSpec as P

SUB = 2
BLK = 128
PAIR = 128
HALF = 64
PAIRS = 6
FIRST = 4
PAY = 2 * BLK + 16
FAR = 1.0e4
SCALE = 0.125
AXES = ("slit", "span")
VMEM = 64 * 1024 * 1024 - 128 * 1024
GRID_A = 64
GRID_B = 16

NT = (((1,), (1,)), ((), ()))
NN = (((1,), (0,)), ((), ()))


def dot(a, b, dims):
    return lax.dot_general(a, b, dims, preferred_element_type=jnp.float32)


def cat(xs, axis):
    return jnp.concatenate(xs, axis=axis) if len(xs) > 1 else xs[0]


def head_masks():
    lane = lax.broadcasted_iota(jnp.int32, (1, PAIR), 1)
    first = jnp.where(lane < HALF, 1.0, 0.0)
    return first.astype(jnp.bfloat16), (1.0 - first).astype(jnp.bfloat16)


def split_heads(x, masks):
    return jnp.concatenate([x * masks[0], x * masks[1]], axis=0)


def offset_row(dr, dc):
    o = (dr + 1) * 3 + dc + 1
    return 8 if o == 4 else (o if o < 4 else o - 1)


def twice(x):
    return jnp.concatenate([x, x], axis=1)


def attend(tasks, masks):
    scored = []
    for (q, do, _, _, _), keys, values, _ in tasks:
        q2 = split_heads(q * jnp.asarray(SCALE, jnp.bfloat16), masks)
        do2 = split_heads(do, masks)
        scored.append((q2, do2, dot(cat(keys, 0), q2, NT), dot(cat(values, 0), do2, NT)))
    weighted = []
    for ((_, _, lse, delta, biases), _, _, _), (_, _, s, dp) in zip(tasks, scored):
        p_parts, g_parts = [], []
        for n, bias in enumerate(biases):
            part = slice(n * BLK, (n + 1) * BLK)
            p = jnp.exp(s[part] - (lse + bias))
            p_parts.append(p.astype(jnp.bfloat16))
            g_parts.append((p * (dp[part] - delta)).astype(jnp.bfloat16))
        weighted.append((cat(p_parts, 0), cat(g_parts, 0)))
    results = []
    for (_, _, _, keys_t), (q2, do2, _, _), (p, g) in zip(tasks, scored, weighted):
        kt = cat(keys_t, 1)
        dv = dot(p, do2, NN)
        dk = dot(g, q2, NN)
        dq_t = jnp.concatenate(
            [dot(kt[:HALF], g[:, :BLK], NN), dot(kt[HALF:], g[:, BLK:], NN)], axis=0
        )
        results.append((dk, dv, dq_t))
    return results


def flip(block):
    return block.astype(jnp.float32).T.astype(jnp.bfloat16)


def by_rows(par, run, together=False):
    middle = [(1, [0, 1, 2]), (2, [1, 2, 3])]
    if not together:
        run(middle)

    for core, ends in enumerate(([(0, [0, 1]), (3, [2, 3, 4])], [(0, [-1, 0, 1]), (3, [2, 3])])):
        pl.when(par == core)(functools.partial(run, middle + ends if together else ends))


def row_sums(do, o):
    prod = do.astype(jnp.float32) * o.astype(jnp.float32)
    high = prod.astype(jnp.bfloat16)
    low = (prod - high.astype(jnp.float32)).astype(jnp.bfloat16)
    shape = (16, do.shape[1])
    row = lax.broadcasted_iota(jnp.int32, shape, 0)
    lane = lax.broadcasted_iota(jnp.int32, shape, 1)
    pick = jnp.where(row == lane // HALF, 1.0, 0.0).astype(jnp.bfloat16)
    return dot(pick, high, NT) + dot(pick, low, NT)


def mark_lists(pos_ref, near_ref, flag_ref, r, c, dst_ref, at):
    dst_ref[at] = jnp.zeros((16, BLK), jnp.float32)
    for e in range(8):
        key = near_ref[r, c, e]
        flag = flag_ref[r, c, e]
        da = key // GRID_B - (pos_ref[1] + r)
        da = jnp.where(da > 1, da - GRID_A, jnp.where(da < -1, da + GRID_A, da))
        db = key % GRID_B - (pos_ref[2] + c)
        o = (da + 1) * 3 + db + 1
        row = jnp.where(o == 4, 8, jnp.where(o > 4, o - 1, o))
        row = jnp.clip(jnp.where(flag != 0, row, 15), 0, 15)
        dst_ref[at + (pl.ds(row, 1),)] = jnp.ones((1, BLK), jnp.float32)


def fill_aux(aux_ref, lse, delta, used):
    for n in range(PAIRS):
        lanes = slice(n * BLK, (n + 1) * BLK)
        heads = slice(2 * n, 2 * n + 2)
        for start, x in ((0, lse[heads]), (4, delta[heads])):
            high = x.astype(jnp.bfloat16).astype(jnp.float32)
            aux_ref[start : start + 2, lanes] = high
            aux_ref[start + 2 : start + 4, lanes] = x - high
        aux_ref[8:16, lanes] = used


def prepare_column_kernel(pos_ref, near_ref, flag_ref, q_ref, do_ref, o_ref, lse_ref, delta_ref, used_ref, *rest, c):
    *col_refs, aux_ref = rest
    delta = row_sums(do_ref[0, 0], o_ref[0, 0])[0 : 2 * PAIRS]
    mark_lists(pos_ref, near_ref, flag_ref, pl.program_id(0), c, used_ref, (0,))
    fill_aux(aux_ref, lse_ref[0, c], delta, used_ref[0, 0:8])
    delta_ref[0] = delta
    start = 0
    for col_ref in col_refs:
        lanes = slice(start, start + col_ref.shape[2])
        start = lanes.stop
        col_ref[0, 0:BLK] = q_ref[0, 0, :, lanes]
        col_ref[0, BLK : 2 * BLK] = do_ref[0, 0, :, lanes]
        col_ref[0, 2 * BLK : PAY] = aux_ref[:, lanes].astype(jnp.bfloat16)


def prepare_row_kernel(pos_ref, near_ref, flag_ref, q_ref, do_ref, o_ref, lse_ref, out_ref, dg0_ref, dg1_ref, used_ref, aux_ref):
    delta = row_sums(do_ref[...].reshape(2 * BLK, FULL), o_ref[...].reshape(2 * BLK, FULL))
    for c, dg_ref in ((0, dg0_ref), (1, dg1_ref)):
        mark_lists(pos_ref, near_ref, flag_ref, 3 * pos_ref[0], c, used_ref, (c,))
        fill_aux(aux_ref.at[c], lse_ref[0, c], delta[0 : 2 * PAIRS, c * BLK : (c + 1) * BLK], used_ref[c, 0:8])
        for dst, at in ((out_ref, c), (dg_ref, 0)):
            dst[at, 0:BLK] = q_ref[0, c]
            dst[at, BLK : 2 * BLK] = do_ref[0, c]
            dst[at, 2 * BLK : PAY] = aux_ref[c].astype(jnp.bfloat16)


def local_kernel(pos_ref, q_ref, do_ref, k_ref, v_ref, ks_ref, lse_ref, delta0_ref, delta1_ref, used0_ref, used1_ref, dk_ref, dv_ref, sk_ref, sv_ref, dq_ref, kt_ref):
    h = pl.program_id(0)
    masks = head_masks()
    for c in range(2):
        lanes = slice(c * BLK, (c + 1) * BLK)
        for r in range(4):
            kt_ref[r, :, lanes] = flip(k_ref[r, c])
        kt_ref[4, :, lanes] = flip(ks_ref[0, c])
    for ref in (dk_ref, dv_ref, sk_ref, sv_ref):
        ref[...] = jnp.zeros_like(ref)

    def one(row, key_rows):
        tasks = []
        for c, delta_ref, used_ref in ((0, delta0_ref, used0_ref), (1, delta1_ref, used1_ref)):
            lse = [lse_ref[row, c, pl.ds(2 * h + i, 1), :] for i in range(2)]
            delta = [delta_ref[row, pl.ds(2 * h + i, 1), :] for i in range(2)]
            keys, values, keys_t, biases = [], [], [], []
            for r in key_rows:
                for kc in range(2):
                    sibling = r in (-1, 4)
                    keys.append(ks_ref[0, kc] if sibling else k_ref[r, kc])
                    values.append(ks_ref[1, kc] if sibling else v_ref[r, kc])
                    keys_t.append(kt_ref[4 if sibling else r, :, kc * BLK : (kc + 1) * BLK])
                    at = offset_row(r - row, kc - c)
                    biases.append(twice((1.0 - used_ref[row, at : at + 1, :]) * FAR))
            query = (q_ref[row, c], do_ref[row, c], cat(lse, 1), cat(delta, 1), biases)
            tasks.append((query, keys, values, keys_t))
        results = attend(tasks, masks)
        dk = results[0][0] + results[1][0]
        dv = results[0][1] + results[1][1]
        for n, r in enumerate(key_rows):
            for kc in range(2):
                part = slice((2 * n + kc) * BLK, (2 * n + kc + 1) * BLK)
                if r in (-1, 4):
                    sk_ref[kc] += dk[part]
                    sv_ref[kc] += dv[part]
                else:
                    dk_ref[r, kc] += dk[part]
                    dv_ref[r, kc] += dv[part]
        for c in range(2):
            dq_ref[row, c] = results[c][2].T * SCALE

    def run(groups):
        for row, key_rows in groups:
            one(row, key_rows)

    by_rows(pos_ref[0], run)


def received(ref, at, lanes, aux, rows):
    lse = aux[0:2] + aux[2:4]
    delta = aux[4:6] + aux[6:8]
    biases = [twice((1.0 - row) * FAR) for row in rows]
    stats = [cat([x[0:1], x[1:2]], 1) for x in (lse, delta)]
    return (ref[at, 0:BLK, lanes], ref[at, BLK : 2 * BLK, lanes], stats[0], stats[1], biases)


def column_kernel(pos_ref, k_ref, v_ref, ks_ref, col_ref, dkp_ref, dvp_ref, skp_ref, svp_ref, *rest, side, sub):
    dk_ref, dv_ref, sib_ref, tail_ref, res_ref, kt_ref, acck_ref, accv_ref, accs_ref = rest[-9:]
    masks = head_masks()
    for n in range(sub):
        lanes = slice(n * PAIR, (n + 1) * PAIR)
        for r in range(4):
            kt_ref[n, :, r * BLK : (r + 1) * BLK] = flip(k_ref[r, 0, :, lanes])
        kt_ref[n, :, 4 * BLK :] = flip(ks_ref[0, 0, :, lanes])
    acck_ref[...] = dkp_ref[:, 0]
    accv_ref[...] = dvp_ref[:, 0]
    accs_ref[0] = skp_ref[0]
    accs_ref[1] = svp_ref[0]

    def run(groups):
        tasks, places = [], []
        for n in range(sub):
            lanes = slice(n * PAIR, (n + 1) * PAIR)
            for row, key_rows in groups:
                aux = col_ref[row, 2 * BLK : PAY, lanes].astype(jnp.float32)
                keys, values, keys_t, rows = [], [], [], []
                for r in key_rows:
                    sibling = r in (-1, 4)
                    keys.append(ks_ref[0, 0, :, lanes] if sibling else k_ref[r, 0, :, lanes])
                    values.append(ks_ref[1, 0, :, lanes] if sibling else v_ref[r, 0, :, lanes])
                    at = 4 * BLK if sibling else r * BLK
                    keys_t.append(kt_ref[n, :, at : at + BLK])
                    at = 8 + offset_row(r - row, 1 - 2 * side)
                    rows.append(aux[at : at + 1])
                tasks.append((received(col_ref, row, lanes, aux, rows), keys, values, keys_t))
                places.append((row, key_rows, lanes))
        for (row, key_rows, lanes), (dk, dv, dq_t) in zip(places, attend(tasks, masks)):
            for n, r in enumerate(key_rows):
                part = slice(n * BLK, (n + 1) * BLK)
                if r in (-1, 4):
                    accs_ref[0, :, lanes] += dk[part]
                    accs_ref[1, :, lanes] += dv[part]
                else:
                    acck_ref[r, :, lanes] += dk[part]
                    accv_ref[r, :, lanes] += dv[part]
            res_ref[row, :, lanes] = (dq_t.T * SCALE).astype(jnp.bfloat16)

    by_rows(pos_ref[0], run, together=True)
    for r in range(4):
        dk_ref[r, 0] = acck_ref[r].astype(jnp.bfloat16)
        dv_ref[r, 0] = accv_ref[r].astype(jnp.bfloat16)
    sib_ref[0] = accs_ref[...].astype(jnp.bfloat16)
    for i in range(2):
        tail_ref[i, 0, 0] = acck_ref[3 * i]
        tail_ref[i, 0, 1] = accv_ref[3 * i]


def outer_kernel(pos_ref, k_ref, v_ref, out_ref, dg0_ref, dg1_ref, part_ref, ro_ref, rg0_ref, rg1_ref):
    masks = head_masks()
    below = pos_ref[0] == 0
    slots = ((dg0_ref, 0, rg0_ref, -1), (out_ref, 0, ro_ref, 0), (out_ref, 1, ro_ref, 1), (dg1_ref, 0, rg1_ref, 2))
    tasks, places = [], []
    for n in range(SUB):
        lanes = slice(n * PAIR, (n + 1) * PAIR)
        kts = [flip(k_ref[0, c, :, lanes]) for c in range(2)]
        for ref, at, res_ref, c in slots:
            near = [kc for kc in range(2) if abs(kc - c) <= 1]
            aux = ref[at, 2 * BLK : PAY, lanes].astype(jnp.float32)
            ups = [8 + kc - c + 1 for kc in near]
            rows = [jnp.where(below, aux[u + 5 : u + 6], aux[u : u + 1]) for u in ups]
            query = received(ref, at, lanes, aux, rows)
            keys = [k_ref[0, kc, :, lanes] for kc in near]
            values = [v_ref[0, kc, :, lanes] for kc in near]
            tasks.append((query, keys, values, [kts[kc] for kc in near]))
            places.append((lanes, at, res_ref, near))
    totals = {}
    for (lanes, at, res_ref, near), (dk, dv, dq_t) in zip(places, attend(tasks, masks)):
        for n, kc in enumerate(near):
            for i, x in enumerate((dk, dv)):
                x = x[n * BLK : (n + 1) * BLK]
                key = (kc, i, lanes.start)
                totals[key] = totals[key] + x if key in totals else x
        res_ref[at, :, lanes] = (dq_t.T * SCALE).astype(jnp.bfloat16)
    for (kc, i, start), x in totals.items():
        part_ref[kc, i, :, start : start + PAIR] = x


def queries_kernel(pos_ref, dq_ref, back_ref, row_ref, corner_ref, *rest):
    res_ref = rest[-1]
    for r in range(2):
        total = dq_ref[r, 0] + back_ref[r].astype(jnp.float32)
        edge = row_ref[0].astype(jnp.float32) + corner_ref[0].astype(jnp.float32)
        outer = 2 * pl.program_id(0) + r == 3 * pos_ref[0]
        res_ref[r, 0] = jnp.where(outer, total + edge, total).astype(jnp.bfloat16)


def edges_kernel(pos_ref, tail_ref, part_ref, sib_ref, dk_in, dv_in, dk_ref, dv_ref):
    outer = pl.program_id(0) == pos_ref[0]
    for c in range(2):
        for i, ref in enumerate((dk_ref, dv_ref)):
            add = jnp.where(outer, part_ref[c, i], sib_ref[c, i].astype(jnp.float32))
            ref[0, c] = (tail_ref[0, c, i] + add).astype(jnp.bfloat16)


def lanes_spec(shape, base=0, at=None):
    at = at or (0,) * (len(shape) - 1)
    return pl.BlockSpec(shape, lambda h, *_: at + (h + base,))


def rows_spec(shape, lane=0):
    return pl.BlockSpec(shape, lambda r, *_: (r,) + (0,) * (len(shape) - 2) + (lane,))


def fixed(shape, lane=0):
    return pl.BlockSpec(shape, lambda *_: (0,) * (len(shape) - 1) + (lane,))


SMEM = pl.BlockSpec(memory_space=pltpu.SMEM)
ANY = pl.BlockSpec(memory_space=pl.ANY)
TILES = (4, 2, BLK, PAIR)
FULL = PAIRS * PAIR


def sds(shape, dtype=jnp.bfloat16):
    return jax.ShapeDtypeStruct(shape, dtype)


def f32s(shape):
    return sds(shape, jnp.float32)


def call(kernel, name, grid, ins, outs, shapes, scratch=(), alias=None):
    return pl.pallas_call(
        kernel,
        grid_spec=pltpu.PrefetchScalarGridSpec(
            num_scalar_prefetch=1, grid=(grid,), in_specs=ins, out_specs=outs, scratch_shapes=scratch
        ),
        out_shape=shapes,
        input_output_aliases=alias or {},
        compiler_params=pltpu.CompilerParams(
            vmem_limit_bytes=VMEM, dimension_semantics=("arbitrary",)
        ),
        cost_estimate=pl.CostEstimate(flops=1, bytes_accessed=1, transcendentals=0),
        name=name,
    )


def prepare_column(pos, lists, q, do, o, lse, c, parts):
    block = pl.BlockSpec((1, 1, BLK, FULL), lambda r, _: (r, c, 0, 0))
    shapes = [(2 * PAIRS, BLK), (16, BLK)] + [(PAY, n * PAIR) for n in parts]
    kinds = [jnp.float32, jnp.float32] + [jnp.bfloat16] * len(parts)
    return call(
        functools.partial(prepare_column_kernel, c=c),
        "prepare_column",
        4,
        [SMEM] * 2 + [block] * 3 + [rows_spec((1, 2, 2 * PAIRS, BLK))],
        [rows_spec((1,) + shape) for shape in shapes],
        [sds((4,) + shape, kind) for shape, kind in zip(shapes, kinds)],
        [pltpu.VMEM((16, FULL), jnp.float32)],
    )(pos, *lists, q, do, o, lse)


def prepare_row(pos, lists, q, do, o, lse):
    outer = lambda shape: pl.BlockSpec(shape, lambda _, p: (3 * p[0], 0, 0, 0))
    shapes = [(2, PAY, FULL), (1, PAY, FULL), (1, PAY, FULL)]
    return call(
        prepare_row_kernel,
        "prepare_row",
        1,
        [SMEM] * 2 + [outer((1, 2, BLK, FULL))] * 3 + [outer((1, 2, 2 * PAIRS, BLK))],
        [fixed(shape) for shape in shapes],
        [sds(shape) for shape in shapes],
        [pltpu.VMEM((2, 16, BLK), jnp.float32), pltpu.VMEM((2, 16, FULL), jnp.float32)],
    )(pos, *lists, q, do, o, lse)


def local(pos, q, do, k, v, ks, lse, deltas, used):
    tiles = f32s((4, 2, BLK, FULL))
    edge = f32s((2, BLK, FULL))
    return call(
        local_kernel,
        "local",
        PAIRS,
        [lanes_spec(TILES)] * 4
        + [lanes_spec((2, 2, BLK, PAIR)), fixed((4, 2, 2 * PAIRS, BLK))]
        + [fixed((4, 2 * PAIRS, BLK))] * 2
        + [fixed((4, 16, BLK))] * 2,
        [lanes_spec(TILES)] * 2 + [lanes_spec((2, BLK, PAIR))] * 2 + [lanes_spec(TILES)],
        [tiles, tiles, edge, edge, tiles],
        [pltpu.VMEM((5, PAIR, 2 * BLK), jnp.bfloat16)],
    )(pos, q, do, k, v, ks, lse, *deltas, *used)


def column(pos, k, v, ks, col, parts, done, base, count, side):
    sub = SUB if count % SUB == 0 else 1
    wide = sub * PAIR
    at = base // sub
    column_of = lanes_spec((4, 1, BLK, wide), at, (0, side, 0))
    return call(
        functools.partial(column_kernel, side=side, sub=sub),
        "column",
        count // sub,
        [column_of] * 2
        + [lanes_spec((2, 1, BLK, wide), at, (0, side, 0)), lanes_spec((4, PAY, wide))]
        + [column_of] * 2
        + [lanes_spec((1, BLK, wide), at, (side, 0))] * 2
        + [ANY] * len(done),
        [column_of] * 2
        + [
            lanes_spec((1, 2, BLK, wide), at, (side, 0, 0)),
            lanes_spec((2, 1, 2, BLK, wide), at, (0, side, 0, 0)),
            lanes_spec((4, BLK, wide)),
        ],
        [sds((4, 2, BLK, FULL))] * 2
        + [sds((2, 2, BLK, FULL)), f32s((2, 2, 2, BLK, FULL)), sds((4, BLK, count * PAIR))],
        [pltpu.VMEM((sub, PAIR, 5 * BLK), jnp.bfloat16)]
        + [pltpu.VMEM((4, BLK, wide), jnp.float32)] * 2
        + [pltpu.VMEM((2, BLK, wide), jnp.float32)],
        alias={9 + i: i for i in range(len(done))},
    )(pos, k, v, ks, col, *parts, *done)


def outers(pos, k, v, out, dg0, dg1):
    sizes = (2, 1, 1)
    wide = SUB * PAIR
    outer = pl.BlockSpec((1, 2, BLK, wide), lambda h, p: (3 * p[0], 0, 0, h))
    return call(
        outer_kernel,
        "outer_rows",
        PAIRS // SUB,
        [outer] * 2 + [lanes_spec((n, PAY, wide)) for n in sizes],
        [lanes_spec((2, 2, BLK, wide))] + [lanes_spec((n, BLK, wide)) for n in sizes],
        [f32s((2, 2, BLK, FULL))] + [sds((n, BLK, FULL)) for n in sizes],
    )(pos, k, v, out, dg0, dg1)


def finish_queries(pos, dqp, back, back_out, corner, done, c, base, count):
    wide = count * PAIR
    lane = base // count
    block = pl.BlockSpec((2, 1, BLK, wide), lambda r, *_: (r, c, 0, lane))
    edge = lambda at: pl.BlockSpec((1, BLK, wide), lambda *_: (at, 0, lane))
    return call(
        queries_kernel,
        "finish_queries",
        2,
        [block, rows_spec((2, BLK, wide)), edge(c), edge(0)] + [ANY] * len(done),
        block,
        sds((4, 2, BLK, FULL)),
        alias={5 + i: i for i in range(len(done))},
    )(pos, dqp, back, back_out, corner, *done)


def finish_edges(pos, tail, part, sib, dk, dv):
    row = pl.BlockSpec((1, 2, BLK, FULL), lambda i, p: (3 * i, 0, 0, 0))
    edge = (2, 2, BLK, FULL)
    return call(
        edges_kernel,
        "finish_edges",
        2,
        [rows_spec((1,) + edge)] + [fixed(edge)] * 2 + [ANY] * 2,
        [row] * 2,
        [sds((4, 2, BLK, FULL))] * 2,
        alias={4: 0, 5: 1},
    )(pos, tail, part, sib, dk, dv)


def pairs_of(rows, cols):
    at = lambda s, p: (s % rows) * cols + p
    outer = lambda s: s + 1 if s % 2 else s - 1
    inner = lambda s: s - 1 if s % 2 else s + 1
    cells = [(s, p) for s in range(rows) for p in range(cols)]
    return {
        "right": [(at(s, p), at(s, p + 1)) for s, p in cells if p + 1 < cols],
        "left": [(at(s, p), at(s, p - 1)) for s, p in cells if p > 0],
        "outer": [(at(s, p), at(outer(s), p)) for s, p in cells],
        "inner": [(at(s, p), at(inner(s), p)) for s, p in cells],
        "outer_right": [(at(s, p), at(outer(s), p + 1)) for s, p in cells if p + 1 < cols],
        "outer_left": [(at(s, p), at(outer(s), p - 1)) for s, p in cells if p > 0],
    }


def after(pos, *others):
    return lax.optimization_barrier((pos,) + others)[0]


def on_device(rows, cols, q, k, v, o, do, lse, neighbours, flags):
    pairs = pairs_of(rows, cols)
    send = lambda x, way: lax.ppermute(x, AXES, pairs[way])
    row = lax.axis_index("slit")
    pos = jnp.stack([row % 2, row * 4, lax.axis_index("span") * 2]).astype(jnp.int32)
    lists = (neighbours, flags)

    out, dg0, dg1 = prepare_row(pos, lists, q, do, o, lse)
    halo_out = send(out, "outer")
    pos = after(pos, out)
    inner = 3 - 3 * (row % 2)
    kv = jnp.concatenate([lax.dynamic_slice_in_dim(x, inner, 1, 0) for x in (k, v)], axis=0)
    ks = send(kv, "inner")
    delta1, used1, col1 = prepare_column(pos, lists, q, do, o, lse, 1, [PAIRS])
    pos = after(pos, delta1)
    delta0, used0, *col0 = prepare_column(pos, lists, q, do, o, lse, 0, [FIRST, PAIRS - FIRST])
    from_left = send(after(col1, halo_out, ks, delta0), "right")
    from_right = [send(after(x, halo_out, ks), "left") for x in col0]
    halo_g0 = send(dg1, "outer_right")
    halo_g1 = send(dg0, "outer_left")
    pos = after(pos, delta0)

    *parts, dqp = local(pos, q, do, k, v, ks, lse, (delta0, delta1), (used0, used1))
    pos = after(pos, dqp)
    part_out, ro, rg0, rg1 = outers(pos, k, v, halo_out, halo_g0, halo_g1)
    back_out = send(ro, "outer")
    back_g1 = send(rg0, "outer_left")
    back_g0 = send(rg1, "outer_right")
    pos = after(pos, ro)
    *done, res0 = column(pos, k, v, ks, from_left, parts, (), 0, PAIRS, 0)
    back1 = send(res0, "left")
    pos = after(pos, res0)
    *done, res1 = column(pos, k, v, ks, from_right[0], parts, done, 0, FIRST, 1)
    back0 = send(res1, "right")
    pos = after(pos, res1, back_out, back_g0, back_g1)
    dk, dv, sib, tail, res2 = column(pos, k, v, ks, from_right[1], parts, done, FIRST, PAIRS - FIRST, 1)
    back0_last = send(after(res2, back1), "right")

    dq = finish_queries(pos, dqp, back1, back_out, back_g1, (), 1, 0, PAIRS)
    back_sib = send(sib, "inner")
    pos = after(pos, dq)
    dk, dv = finish_edges(pos, tail, part_out, back_sib, dk, dv)
    pos = after(pos, dk)
    dq = finish_queries(pos, dqp, back0, back_out, back_g0, (dq,), 0, 0, FIRST)
    dq = finish_queries(pos, dqp, back0_last, back_out, back_g0, (dq,), 0, FIRST, PAIRS - FIRST)
    return dq, dk, dv


def solution(mesh):
    tile = P("slit", "span", None, None)
    row = P("slit", "span", None)
    body = functools.partial(on_device, mesh.shape["slit"], mesh.shape["span"])
    return jax.shard_map(
        body,
        mesh=mesh,
        in_specs=(tile,) * 6 + (row,) * 2,
        out_specs=(tile,) * 3,
        check_vma=False,
    )
```

```python
import functools

import jax
import jax.numpy as jnp
from jax import lax
from jax.experimental import pallas as pl
from jax.experimental.pallas import tpu as pltpu
from jax.sharding import PartitionSpec as P

SUB = 2
BLK = 128
PAIR = 128
HALF = 64
PAIRS = 6
FIRST = 4
PAY = 2 * BLK + 16
FAR = 1.0e4
SCALE = 0.125
AXES = ("slit", "span")
VMEM = 64 * 1024 * 1024 - 128 * 1024
GRID_A = 64
GRID_B = 16

NT = (((1,), (1,)), ((), ()))
NN = (((1,), (0,)), ((), ()))


def dot(a, b, dims):
    return lax.dot_general(a, b, dims, preferred_element_type=jnp.float32)


def cat(xs, axis):
    return jnp.concatenate(xs, axis=axis) if len(xs) > 1 else xs[0]


def head_masks():
    lane = lax.broadcasted_iota(jnp.int32, (1, PAIR), 1)
    first = jnp.where(lane < HALF, 1.0, 0.0)
    return first.astype(jnp.bfloat16), (1.0 - first).astype(jnp.bfloat16)


def split_heads(x, masks):
    return jnp.concatenate([x * masks[0], x * masks[1]], axis=0)


def offset_row(dr, dc):
    o = (dr + 1) * 3 + dc + 1
    return 8 if o == 4 else (o if o < 4 else o - 1)


def twice(x):
    return jnp.concatenate([x, x], axis=1)


def attend(tasks, masks):
    scored = []
    for (q, do, _, _, _), keys, values, _ in tasks:
        q2 = split_heads(q * jnp.asarray(SCALE, jnp.bfloat16), masks)
        do2 = split_heads(do, masks)
        scored.append((q2, do2, dot(cat(keys, 0), q2, NT), dot(cat(values, 0), do2, NT)))
    weighted = []
    for ((_, _, lse, delta, biases), _, _, _), (_, _, s, dp) in zip(tasks, scored):
        p_parts, g_parts = [], []
        for n, bias in enumerate(biases):
            part = slice(n * BLK, (n + 1) * BLK)
            p = jnp.exp(s[part] - (lse + bias))
            p_parts.append(p.astype(jnp.bfloat16))
            g_parts.append((p * (dp[part] - delta)).astype(jnp.bfloat16))
        weighted.append((cat(p_parts, 0), cat(g_parts, 0)))
    results = []
    for (_, _, _, keys_t), (q2, do2, _, _), (p, g) in zip(tasks, scored, weighted):
        kt = cat(keys_t, 1)
        dv = dot(p, do2, NN)
        dk = dot(g, q2, NN)
        dq_t = jnp.concatenate(
            [dot(kt[:HALF], g[:, :BLK], NN), dot(kt[HALF:], g[:, BLK:], NN)], axis=0
        )
        results.append((dk, dv, dq_t))
    return results


def flip(block):
    return block.astype(jnp.float32).T.astype(jnp.bfloat16)


def by_rows(par, run, together=False):
    middle = [(1, [0, 1, 2]), (2, [1, 2, 3])]
    if not together:
        run(middle)

    for core, ends in enumerate(([(0, [0, 1]), (3, [2, 3, 4])], [(0, [-1, 0, 1]), (3, [2, 3])])):
        pl.when(par == core)(functools.partial(run, middle + ends if together else ends))


def row_sums(do, o):
    prod = do.astype(jnp.float32) * o.astype(jnp.float32)
    high = prod.astype(jnp.bfloat16)
    low = (prod - high.astype(jnp.float32)).astype(jnp.bfloat16)
    shape = (16, do.shape[1])
    row = lax.broadcasted_iota(jnp.int32, shape, 0)
    lane = lax.broadcasted_iota(jnp.int32, shape, 1)
    pick = jnp.where(row == lane // HALF, 1.0, 0.0).astype(jnp.bfloat16)
    return dot(pick, high, NT) + dot(pick, low, NT)


def mark_lists(pos_ref, near_ref, flag_ref, r, c, dst_ref, at):
    dst_ref[at] = jnp.zeros((16, BLK), jnp.float32)
    for e in range(8):
        key = near_ref[r, c, e]
        flag = flag_ref[r, c, e]
        da = key // GRID_B - (pos_ref[1] + r)
        da = jnp.where(da > 1, da - GRID_A, jnp.where(da < -1, da + GRID_A, da))
        db = key % GRID_B - (pos_ref[2] + c)
        o = (da + 1) * 3 + db + 1
        row = jnp.where(o == 4, 8, jnp.where(o > 4, o - 1, o))
        row = jnp.clip(jnp.where(flag != 0, row, 15), 0, 15)
        dst_ref[at + (pl.ds(row, 1),)] = jnp.ones((1, BLK), jnp.float32)


def fill_aux(aux_ref, lse, delta, used):
    for n in range(PAIRS):
        lanes = slice(n * BLK, (n + 1) * BLK)
        heads = slice(2 * n, 2 * n + 2)
        for start, x in ((0, lse[heads]), (4, delta[heads])):
            high = x.astype(jnp.bfloat16).astype(jnp.float32)
            aux_ref[start : start + 2, lanes] = high
            aux_ref[start + 2 : start + 4, lanes] = x - high
        aux_ref[8:16, lanes] = used


def prepare_column_kernel(pos_ref, near_ref, flag_ref, q_ref, do_ref, o_ref, lse_ref, delta_ref, used_ref, *rest, c):
    *col_refs, aux_ref = rest
    delta = row_sums(do_ref[0, 0], o_ref[0, 0])[0 : 2 * PAIRS]
    mark_lists(pos_ref, near_ref, flag_ref, pl.program_id(0), c, used_ref, (0,))
    fill_aux(aux_ref, lse_ref[0, c], delta, used_ref[0, 0:8])
    delta_ref[0] = delta
    start = 0
    for col_ref in col_refs:
        lanes = slice(start, start + col_ref.shape[2])
        start = lanes.stop
        col_ref[0, 0:BLK] = q_ref[0, 0, :, lanes]
        col_ref[0, BLK : 2 * BLK] = do_ref[0, 0, :, lanes]
        col_ref[0, 2 * BLK : PAY] = aux_ref[:, lanes].astype(jnp.bfloat16)


def prepare_row_kernel(pos_ref, near_ref, flag_ref, q_ref, do_ref, o_ref, lse_ref, out_ref, dg0_ref, dg1_ref, used_ref, aux_ref):
    delta = row_sums(do_ref[...].reshape(2 * BLK, FULL), o_ref[...].reshape(2 * BLK, FULL))
    for c, dg_ref in ((0, dg0_ref), (1, dg1_ref)):
        mark_lists(pos_ref, near_ref, flag_ref, 3 * pos_ref[0], c, used_ref, (c,))
        fill_aux(aux_ref.at[c], lse_ref[0, c], delta[0 : 2 * PAIRS, c * BLK : (c + 1) * BLK], used_ref[c, 0:8])
        for dst, at in ((out_ref, c), (dg_ref, 0)):
            dst[at, 0:BLK] = q_ref[0, c]
            dst[at, BLK : 2 * BLK] = do_ref[0, c]
            dst[at, 2 * BLK : PAY] = aux_ref[c].astype(jnp.bfloat16)


def local_kernel(pos_ref, q_ref, do_ref, k_ref, v_ref, ks_ref, lse_ref, delta0_ref, delta1_ref, used0_ref, used1_ref, dk_ref, dv_ref, sk_ref, sv_ref, dq_ref, kt_ref):
    h = pl.program_id(0)
    masks = head_masks()
    for c in range(2):
        lanes = slice(c * BLK, (c + 1) * BLK)
        for r in range(4):
            kt_ref[r, :, lanes] = flip(k_ref[r, c])
        kt_ref[4, :, lanes] = flip(ks_ref[0, c])
    for ref in (dk_ref, dv_ref, sk_ref, sv_ref):
        ref[...] = jnp.zeros_like(ref)

    def one(row, key_rows):
        tasks = []
        for c, delta_ref, used_ref in ((0, delta0_ref, used0_ref), (1, delta1_ref, used1_ref)):
            lse = [lse_ref[row, c, pl.ds(2 * h + i, 1), :] for i in range(2)]
            delta = [delta_ref[row, pl.ds(2 * h + i, 1), :] for i in range(2)]
            keys, values, keys_t, biases = [], [], [], []
            for r in key_rows:
                for kc in range(2):
                    sibling = r in (-1, 4)
                    keys.append(ks_ref[0, kc] if sibling else k_ref[r, kc])
                    values.append(ks_ref[1, kc] if sibling else v_ref[r, kc])
                    keys_t.append(kt_ref[4 if sibling else r, :, kc * BLK : (kc + 1) * BLK])
                    at = offset_row(r - row, kc - c)
                    biases.append(twice((1.0 - used_ref[row, at : at + 1, :]) * FAR))
            query = (q_ref[row, c], do_ref[row, c], cat(lse, 1), cat(delta, 1), biases)
            tasks.append((query, keys, values, keys_t))
        results = attend(tasks, masks)
        dk = results[0][0] + results[1][0]
        dv = results[0][1] + results[1][1]
        for n, r in enumerate(key_rows):
            for kc in range(2):
                part = slice((2 * n + kc) * BLK, (2 * n + kc + 1) * BLK)
                if r in (-1, 4):
                    sk_ref[kc] += dk[part]
                    sv_ref[kc] += dv[part]
                else:
                    dk_ref[r, kc] += dk[part]
                    dv_ref[r, kc] += dv[part]
        for c in range(2):
            dq_ref[row, c] = results[c][2].T * SCALE

    def run(groups):
        for row, key_rows in groups:
            one(row, key_rows)

    by_rows(pos_ref[0], run)


def received(ref, at, lanes, aux, rows):
    lse = aux[0:2] + aux[2:4]
    delta = aux[4:6] + aux[6:8]
    biases = [twice((1.0 - row) * FAR) for row in rows]
    stats = [cat([x[0:1], x[1:2]], 1) for x in (lse, delta)]
    return (ref[at, 0:BLK, lanes], ref[at, BLK : 2 * BLK, lanes], stats[0], stats[1], biases)


def column_kernel(pos_ref, k_ref, v_ref, ks_ref, col_ref, dkp_ref, dvp_ref, skp_ref, svp_ref, *rest, side, sub):
    dk_ref, dv_ref, sib_ref, tail_ref, res_ref, kt_ref, acck_ref, accv_ref, accs_ref = rest[-9:]
    masks = head_masks()
    for n in range(sub):
        lanes = slice(n * PAIR, (n + 1) * PAIR)
        for r in range(4):
            kt_ref[n, :, r * BLK : (r + 1) * BLK] = flip(k_ref[r, 0, :, lanes])
        kt_ref[n, :, 4 * BLK :] = flip(ks_ref[0, 0, :, lanes])
    acck_ref[...] = dkp_ref[:, 0]
    accv_ref[...] = dvp_ref[:, 0]
    accs_ref[0] = skp_ref[0]
    accs_ref[1] = svp_ref[0]

    def run(groups):
        tasks, places = [], []
        for n in range(sub):
            lanes = slice(n * PAIR, (n + 1) * PAIR)
            for row, key_rows in groups:
                aux = col_ref[row, 2 * BLK : PAY, lanes].astype(jnp.float32)
                keys, values, keys_t, rows = [], [], [], []
                for r in key_rows:
                    sibling = r in (-1, 4)
                    keys.append(ks_ref[0, 0, :, lanes] if sibling else k_ref[r, 0, :, lanes])
                    values.append(ks_ref[1, 0, :, lanes] if sibling else v_ref[r, 0, :, lanes])
                    at = 4 * BLK if sibling else r * BLK
                    keys_t.append(kt_ref[n, :, at : at + BLK])
                    at = 8 + offset_row(r - row, 1 - 2 * side)
                    rows.append(aux[at : at + 1])
                tasks.append((received(col_ref, row, lanes, aux, rows), keys, values, keys_t))
                places.append((row, key_rows, lanes))
        for (row, key_rows, lanes), (dk, dv, dq_t) in zip(places, attend(tasks, masks)):
            for n, r in enumerate(key_rows):
                part = slice(n * BLK, (n + 1) * BLK)
                if r in (-1, 4):
                    accs_ref[0, :, lanes] += dk[part]
                    accs_ref[1, :, lanes] += dv[part]
                else:
                    acck_ref[r, :, lanes] += dk[part]
                    accv_ref[r, :, lanes] += dv[part]
            res_ref[row, :, lanes] = (dq_t.T * SCALE).astype(jnp.bfloat16)

    by_rows(pos_ref[0], run, together=True)
    for r in range(4):
        dk_ref[r, 0] = acck_ref[r].astype(jnp.bfloat16)
        dv_ref[r, 0] = accv_ref[r].astype(jnp.bfloat16)
    sib_ref[0] = accs_ref[...].astype(jnp.bfloat16)
    for i in range(2):
        tail_ref[i, 0, 0] = acck_ref[3 * i]
        tail_ref[i, 0, 1] = accv_ref[3 * i]


def outer_kernel(pos_ref, k_ref, v_ref, out_ref, dg0_ref, dg1_ref, part_ref, ro_ref, rg0_ref, rg1_ref):
    masks = head_masks()
    below = pos_ref[0] == 0
    slots = ((dg0_ref, 0, rg0_ref, -1), (out_ref, 0, ro_ref, 0), (out_ref, 1, ro_ref, 1), (dg1_ref, 0, rg1_ref, 2))
    tasks, places = [], []
    for n in range(SUB):
        lanes = slice(n * PAIR, (n + 1) * PAIR)
        kts = [flip(k_ref[0, c, :, lanes]) for c in range(2)]
        for ref, at, res_ref, c in slots:
            near = [kc for kc in range(2) if abs(kc - c) <= 1]
            aux = ref[at, 2 * BLK : PAY, lanes].astype(jnp.float32)
            ups = [8 + kc - c + 1 for kc in near]
            rows = [jnp.where(below, aux[u + 5 : u + 6], aux[u : u + 1]) for u in ups]
            query = received(ref, at, lanes, aux, rows)
            keys = [k_ref[0, kc, :, lanes] for kc in near]
            values = [v_ref[0, kc, :, lanes] for kc in near]
            tasks.append((query, keys, values, [kts[kc] for kc in near]))
            places.append((lanes, at, res_ref, near))
    totals = {}
    for (lanes, at, res_ref, near), (dk, dv, dq_t) in zip(places, attend(tasks, masks)):
        for n, kc in enumerate(near):
            for i, x in enumerate((dk, dv)):
                x = x[n * BLK : (n + 1) * BLK]
                key = (kc, i, lanes.start)
                totals[key] = totals[key] + x if key in totals else x
        res_ref[at, :, lanes] = (dq_t.T * SCALE).astype(jnp.bfloat16)
    for (kc, i, start), x in totals.items():
        part_ref[kc, i, :, start : start + PAIR] = x


def queries_kernel(pos_ref, dq_ref, back_ref, row_ref, corner_ref, *rest):
    res_ref = rest[-1]
    for r in range(2):
        total = dq_ref[r, 0] + back_ref[r].astype(jnp.float32)
        edge = row_ref[0].astype(jnp.float32) + corner_ref[0].astype(jnp.float32)
        outer = 2 * pl.program_id(0) + r == 3 * pos_ref[0]
        res_ref[r, 0] = jnp.where(outer, total + edge, total).astype(jnp.bfloat16)


def edges_kernel(pos_ref, tail_ref, part_ref, sib_ref, dk_in, dv_in, dk_ref, dv_ref):
    outer = pl.program_id(0) == pos_ref[0]
    for c in range(2):
        for i, ref in enumerate((dk_ref, dv_ref)):
            add = jnp.where(outer, part_ref[c, i], sib_ref[c, i].astype(jnp.float32))
            ref[0, c] = (tail_ref[0, c, i] + add).astype(jnp.bfloat16)


def lanes_spec(shape, base=0, at=None):
    at = at or (0,) * (len(shape) - 1)
    return pl.BlockSpec(shape, lambda h, *_: at + (h + base,))


def rows_spec(shape, lane=0):
    return pl.BlockSpec(shape, lambda r, *_: (r,) + (0,) * (len(shape) - 2) + (lane,))


def fixed(shape, lane=0):
    return pl.BlockSpec(shape, lambda *_: (0,) * (len(shape) - 1) + (lane,))


SMEM = pl.BlockSpec(memory_space=pltpu.SMEM)
ANY = pl.BlockSpec(memory_space=pl.ANY)
TILES = (4, 2, BLK, PAIR)
FULL = PAIRS * PAIR


def sds(shape, dtype=jnp.bfloat16):
    return jax.ShapeDtypeStruct(shape, dtype)


def f32s(shape):
    return sds(shape, jnp.float32)


def call(kernel, name, grid, ins, outs, shapes, scratch=(), alias=None):
    return pl.pallas_call(
        kernel,
        grid_spec=pltpu.PrefetchScalarGridSpec(
            num_scalar_prefetch=1, grid=(grid,), in_specs=ins, out_specs=outs, scratch_shapes=scratch
        ),
        out_shape=shapes,
        input_output_aliases=alias or {},
        compiler_params=pltpu.CompilerParams(
            vmem_limit_bytes=VMEM, dimension_semantics=("arbitrary",)
        ),
        cost_estimate=pl.CostEstimate(flops=1, bytes_accessed=1, transcendentals=0),
        name=name,
    )


def prepare_column(pos, lists, q, do, o, lse, c, parts):
    block = pl.BlockSpec((1, 1, BLK, FULL), lambda r, _: (r, c, 0, 0))
    shapes = [(2 * PAIRS, BLK), (16, BLK)] + [(PAY, n * PAIR) for n in parts]
    kinds = [jnp.float32, jnp.float32] + [jnp.bfloat16] * len(parts)
    return call(
        functools.partial(prepare_column_kernel, c=c),
        "prepare_column",
        4,
        [SMEM] * 2 + [block] * 3 + [rows_spec((1, 2, 2 * PAIRS, BLK))],
        [rows_spec((1,) + shape) for shape in shapes],
        [sds((4,) + shape, kind) for shape, kind in zip(shapes, kinds)],
        [pltpu.VMEM((16, FULL), jnp.float32)],
    )(pos, *lists, q, do, o, lse)


def prepare_row(pos, lists, q, do, o, lse):
    outer = lambda shape: pl.BlockSpec(shape, lambda _, p: (3 * p[0], 0, 0, 0))
    shapes = [(2, PAY, FULL), (1, PAY, FULL), (1, PAY, FULL)]
    return call(
        prepare_row_kernel,
        "prepare_row",
        1,
        [SMEM] * 2 + [outer((1, 2, BLK, FULL))] * 3 + [outer((1, 2, 2 * PAIRS, BLK))],
        [fixed(shape) for shape in shapes],
        [sds(shape) for shape in shapes],
        [pltpu.VMEM((2, 16, BLK), jnp.float32), pltpu.VMEM((2, 16, FULL), jnp.float32)],
    )(pos, *lists, q, do, o, lse)


def local(pos, q, do, k, v, ks, lse, deltas, used):
    tiles = f32s((4, 2, BLK, FULL))
    edge = f32s((2, BLK, FULL))
    return call(
        local_kernel,
        "local",
        PAIRS,
        [lanes_spec(TILES)] * 4
        + [lanes_spec((2, 2, BLK, PAIR)), fixed((4, 2, 2 * PAIRS, BLK))]
        + [fixed((4, 2 * PAIRS, BLK))] * 2
        + [fixed((4, 16, BLK))] * 2,
        [lanes_spec(TILES)] * 2 + [lanes_spec((2, BLK, PAIR))] * 2 + [lanes_spec(TILES)],
        [tiles, tiles, edge, edge, tiles],
        [pltpu.VMEM((5, PAIR, 2 * BLK), jnp.bfloat16)],
    )(pos, q, do, k, v, ks, lse, *deltas, *used)


def column(pos, k, v, ks, col, parts, done, base, count, side):
    sub = SUB if count % SUB == 0 else 1
    wide = sub * PAIR
    at = base // sub
    column_of = lanes_spec((4, 1, BLK, wide), at, (0, side, 0))
    return call(
        functools.partial(column_kernel, side=side, sub=sub),
        "column",
        count // sub,
        [column_of] * 2
        + [lanes_spec((2, 1, BLK, wide), at, (0, side, 0)), lanes_spec((4, PAY, wide))]
        + [column_of] * 2
        + [lanes_spec((1, BLK, wide), at, (side, 0))] * 2
        + [ANY] * len(done),
        [column_of] * 2
        + [
            lanes_spec((1, 2, BLK, wide), at, (side, 0, 0)),
            lanes_spec((2, 1, 2, BLK, wide), at, (0, side, 0, 0)),
            lanes_spec((4, BLK, wide)),
        ],
        [sds((4, 2, BLK, FULL))] * 2
        + [sds((2, 2, BLK, FULL)), f32s((2, 2, 2, BLK, FULL)), sds((4, BLK, count * PAIR))],
        [pltpu.VMEM((sub, PAIR, 5 * BLK), jnp.bfloat16)]
        + [pltpu.VMEM((4, BLK, wide), jnp.float32)] * 2
        + [pltpu.VMEM((2, BLK, wide), jnp.float32)],
        alias={9 + i: i for i in range(len(done))},
    )(pos, k, v, ks, col, *parts, *done)


def outers(pos, k, v, out, dg0, dg1):
    sizes = (2, 1, 1)
    wide = SUB * PAIR
    outer = pl.BlockSpec((1, 2, BLK, wide), lambda h, p: (3 * p[0], 0, 0, h))
    return call(
        outer_kernel,
        "outer_rows",
        PAIRS // SUB,
        [outer] * 2 + [lanes_spec((n, PAY, wide)) for n in sizes],
        [lanes_spec((2, 2, BLK, wide))] + [lanes_spec((n, BLK, wide)) for n in sizes],
        [f32s((2, 2, BLK, FULL))] + [sds((n, BLK, FULL)) for n in sizes],
    )(pos, k, v, out, dg0, dg1)


def finish_queries(pos, dqp, back, back_out, corner, done, c, base, count):
    wide = count * PAIR
    lane = base // count
    block = pl.BlockSpec((2, 1, BLK, wide), lambda r, *_: (r, c, 0, lane))
    edge = lambda at: pl.BlockSpec((1, BLK, wide), lambda *_: (at, 0, lane))
    return call(
        queries_kernel,
        "finish_queries",
        2,
        [block, rows_spec((2, BLK, wide)), edge(c), edge(0)] + [ANY] * len(done),
        block,
        sds((4, 2, BLK, FULL)),
        alias={5 + i: i for i in range(len(done))},
    )(pos, dqp, back, back_out, corner, *done)


def finish_edges(pos, tail, part, sib, dk, dv):
    row = pl.BlockSpec((1, 2, BLK, FULL), lambda i, p: (3 * i, 0, 0, 0))
    edge = (2, 2, BLK, FULL)
    return call(
        edges_kernel,
        "finish_edges",
        2,
        [rows_spec((1,) + edge)] + [fixed(edge)] * 2 + [ANY] * 2,
        [row] * 2,
        [sds((4, 2, BLK, FULL))] * 2,
        alias={4: 0, 5: 1},
    )(pos, tail, part, sib, dk, dv)


def pairs_of(rows, cols):
    at = lambda s, p: (s % rows) * cols + p
    outer = lambda s: s + 1 if s % 2 else s - 1
    inner = lambda s: s - 1 if s % 2 else s + 1
    cells = [(s, p) for s in range(rows) for p in range(cols)]
    return {
        "right": [(at(s, p), at(s, p + 1)) for s, p in cells if p + 1 < cols],
        "left": [(at(s, p), at(s, p - 1)) for s, p in cells if p > 0],
        "outer": [(at(s, p), at(outer(s), p)) for s, p in cells],
        "inner": [(at(s, p), at(inner(s), p)) for s, p in cells],
        "outer_right": [(at(s, p), at(outer(s), p + 1)) for s, p in cells if p + 1 < cols],
        "outer_left": [(at(s, p), at(outer(s), p - 1)) for s, p in cells if p > 0],
    }


def after(pos, *others):
    return lax.optimization_barrier((pos,) + others)[0]


def on_device(rows, cols, q, k, v, o, do, lse, neighbours, flags):
    pairs = pairs_of(rows, cols)
    send = lambda x, way: lax.ppermute(x, AXES, pairs[way])
    row = lax.axis_index("slit")
    pos = jnp.stack([row % 2, row * 4, lax.axis_index("span") * 2]).astype(jnp.int32)
    lists = (neighbours, flags)

    out, dg0, dg1 = prepare_row(pos, lists, q, do, o, lse)
    halo_out = send(out, "outer")
    pos = after(pos, out)
    inner = 3 - 3 * (row % 2)
    kv = jnp.concatenate([lax.dynamic_slice_in_dim(x, inner, 1, 0) for x in (k, v)], axis=0)
    ks = send(kv, "inner")
    delta1, used1, col1 = prepare_column(pos, lists, q, do, o, lse, 1, [PAIRS])
    pos = after(pos, delta1)
    delta0, used0, *col0 = prepare_column(pos, lists, q, do, o, lse, 0, [FIRST, PAIRS - FIRST])
    from_left = send(after(col1, ks), "right")
    halo_g0 = send(dg1, "outer_right")
    halo_g1 = send(dg0, "outer_left")
    ready = (halo_out, ks, halo_g0, halo_g1)
    from_right = [send(after(x, *ready), "left") for x in col0]
    pos = after(pos, delta0)

    *parts, dqp = local(pos, q, do, k, v, ks, lse, (delta0, delta1), (used0, used1))
    pos = after(pos, dqp)
    part_out, ro, rg0, rg1 = outers(pos, k, v, halo_out, halo_g0, halo_g1)
    back_out = send(ro, "outer")
    back_g1 = send(rg0, "outer_left")
    back_g0 = send(rg1, "outer_right")
    pos = after(pos, ro)
    *done, res0 = column(pos, k, v, ks, from_left, parts, (), 0, PAIRS, 0)
    back1 = send(res0, "left")
    pos = after(pos, res0)
    *done, res1 = column(pos, k, v, ks, from_right[0], parts, done, 0, FIRST, 1)
    back0 = send(res1, "right")
    pos = after(pos, res1, back_out, back_g0, back_g1)
    dk, dv, sib, tail, res2 = column(pos, k, v, ks, from_right[1], parts, done, FIRST, PAIRS - FIRST, 1)
    back0_last = send(after(res2, back1), "right")

    dq = finish_queries(pos, dqp, back1, back_out, back_g1, (), 1, 0, PAIRS)
    back_sib = send(sib, "inner")
    pos = after(pos, dq)
    dk, dv = finish_edges(pos, tail, part_out, back_sib, dk, dv)
    pos = after(pos, dk)
    dq = finish_queries(pos, dqp, back0, back_out, back_g0, (dq,), 0, 0, FIRST)
    dq = finish_queries(pos, dqp, back0_last, back_out, back_g0, (dq,), 0, FIRST, PAIRS - FIRST)
    return dq, dk, dv


def solution(mesh):
    tile = P("slit", "span", None, None)
    row = P("slit", "span", None)
    body = functools.partial(on_device, mesh.shape["slit"], mesh.shape["span"])
    return jax.shard_map(
        body,
        mesh=mesh,
        in_specs=(tile,) * 6 + (row,) * 2,
        out_specs=(tile,) * 3,
        check_vma=False,
    )
```

```python
import functools

import jax
import jax.numpy as jnp
from jax import lax
from jax.experimental import pallas as pl
from jax.experimental.pallas import tpu as pltpu
from jax.sharding import PartitionSpec as P

SUB = 2
BLK = 128
PAIR = 128
HALF = 64
PAIRS = 6
FIRST = 4
PAY = 2 * BLK + 16
FAR = 1.0e4
SCALE = 0.125
AXES = ("slit", "span")
VMEM = 64 * 1024 * 1024 - 128 * 1024
GRID_A = 64
GRID_B = 16

NT = (((1,), (1,)), ((), ()))
NN = (((1,), (0,)), ((), ()))


def dot(a, b, dims):
    return lax.dot_general(a, b, dims, preferred_element_type=jnp.float32)


def cat(xs, axis):
    return jnp.concatenate(xs, axis=axis) if len(xs) > 1 else xs[0]


def head_masks():
    lane = lax.broadcasted_iota(jnp.int32, (1, PAIR), 1)
    first = jnp.where(lane < HALF, 1.0, 0.0)
    return first.astype(jnp.bfloat16), (1.0 - first).astype(jnp.bfloat16)


def split_heads(x, masks):
    return jnp.concatenate([x * masks[0], x * masks[1]], axis=0)


def offset_row(dr, dc):
    o = (dr + 1) * 3 + dc + 1
    return 8 if o == 4 else (o if o < 4 else o - 1)


def twice(x):
    return jnp.concatenate([x, x], axis=1)


def attend(tasks, masks):
    scored = []
    for (q, do, _, _, _), keys, values, _ in tasks:
        q2 = split_heads(q * jnp.asarray(SCALE, jnp.bfloat16), masks)
        do2 = split_heads(do, masks)
        scored.append((q2, do2, dot(cat(keys, 0), q2, NT), dot(cat(values, 0), do2, NT)))
    weighted = []
    for ((_, _, lse, delta, biases), _, _, _), (_, _, s, dp) in zip(tasks, scored):
        p_parts, g_parts = [], []
        for n, bias in enumerate(biases):
            part = slice(n * BLK, (n + 1) * BLK)
            p = jnp.exp(s[part] - (lse + bias))
            p_parts.append(p.astype(jnp.bfloat16))
            g_parts.append((p * (dp[part] - delta)).astype(jnp.bfloat16))
        weighted.append((cat(p_parts, 0), cat(g_parts, 0)))
    results = []
    for (_, _, _, keys_t), (q2, do2, _, _), (p, g) in zip(tasks, scored, weighted):
        kt = cat(keys_t, 1)
        dv = dot(p, do2, NN)
        dk = dot(g, q2, NN)
        dq_t = jnp.concatenate(
            [dot(kt[:HALF], g[:, :BLK], NN), dot(kt[HALF:], g[:, BLK:], NN)], axis=0
        )
        results.append((dk, dv, dq_t))
    return results


def flip(block):
    return block.astype(jnp.float32).T.astype(jnp.bfloat16)


def by_rows(par, run, together=False):
    middle = [(1, [0, 1, 2]), (2, [1, 2, 3])]
    if not together:
        run(middle)

    for core, ends in enumerate(([(0, [0, 1]), (3, [2, 3, 4])], [(0, [-1, 0, 1]), (3, [2, 3])])):
        pl.when(par == core)(functools.partial(run, middle + ends if together else ends))


def row_sums(do, o):
    prod = do.astype(jnp.float32) * o.astype(jnp.float32)
    high = prod.astype(jnp.bfloat16)
    low = (prod - high.astype(jnp.float32)).astype(jnp.bfloat16)
    shape = (16, do.shape[1])
    row = lax.broadcasted_iota(jnp.int32, shape, 0)
    lane = lax.broadcasted_iota(jnp.int32, shape, 1)
    pick = jnp.where(row == lane // HALF, 1.0, 0.0).astype(jnp.bfloat16)
    return dot(pick, high, NT) + dot(pick, low, NT)


def mark_lists(pos_ref, near_ref, flag_ref, r, c, dst_ref, at):
    dst_ref[at] = jnp.zeros((16, BLK), jnp.float32)
    for e in range(8):
        key = near_ref[r, c, e]
        flag = flag_ref[r, c, e]
        da = key // GRID_B - (pos_ref[1] + r)
        da = jnp.where(da > 1, da - GRID_A, jnp.where(da < -1, da + GRID_A, da))
        db = key % GRID_B - (pos_ref[2] + c)
        o = (da + 1) * 3 + db + 1
        row = jnp.where(o == 4, 8, jnp.where(o > 4, o - 1, o))
        row = jnp.clip(jnp.where(flag != 0, row, 15), 0, 15)
        dst_ref[at + (pl.ds(row, 1),)] = jnp.ones((1, BLK), jnp.float32)


def fill_aux(aux_ref, lse, delta, used):
    for n in range(PAIRS):
        lanes = slice(n * BLK, (n + 1) * BLK)
        heads = slice(2 * n, 2 * n + 2)
        for start, x in ((0, lse[heads]), (4, delta[heads])):
            high = x.astype(jnp.bfloat16).astype(jnp.float32)
            aux_ref[start : start + 2, lanes] = high
            aux_ref[start + 2 : start + 4, lanes] = x - high
        aux_ref[8:16, lanes] = used


def prepare_column_kernel(pos_ref, near_ref, flag_ref, q_ref, do_ref, o_ref, lse_ref, delta_ref, used_ref, *rest, c):
    *col_refs, aux_ref = rest
    delta = row_sums(do_ref[0, 0], o_ref[0, 0])[0 : 2 * PAIRS]
    mark_lists(pos_ref, near_ref, flag_ref, pl.program_id(0), c, used_ref, (0,))
    fill_aux(aux_ref, lse_ref[0, c], delta, used_ref[0, 0:8])
    delta_ref[0] = delta
    start = 0
    for col_ref in col_refs:
        lanes = slice(start, start + col_ref.shape[2])
        start = lanes.stop
        col_ref[0, 0:BLK] = q_ref[0, 0, :, lanes]
        col_ref[0, BLK : 2 * BLK] = do_ref[0, 0, :, lanes]
        col_ref[0, 2 * BLK : PAY] = aux_ref[:, lanes].astype(jnp.bfloat16)


def prepare_row_kernel(pos_ref, near_ref, flag_ref, q_ref, do_ref, o_ref, lse_ref, out_ref, dg0_ref, dg1_ref, used_ref, aux_ref):
    delta = row_sums(do_ref[...].reshape(2 * BLK, FULL), o_ref[...].reshape(2 * BLK, FULL))
    for c, dg_ref in ((0, dg0_ref), (1, dg1_ref)):
        mark_lists(pos_ref, near_ref, flag_ref, 3 * pos_ref[0], c, used_ref, (c,))
        fill_aux(aux_ref.at[c], lse_ref[0, c], delta[0 : 2 * PAIRS, c * BLK : (c + 1) * BLK], used_ref[c, 0:8])
        for dst, at in ((out_ref, c), (dg_ref, 0)):
            dst[at, 0:BLK] = q_ref[0, c]
            dst[at, BLK : 2 * BLK] = do_ref[0, c]
            dst[at, 2 * BLK : PAY] = aux_ref[c].astype(jnp.bfloat16)


def local_kernel(pos_ref, q_ref, do_ref, k_ref, v_ref, ks_ref, lse_ref, delta0_ref, delta1_ref, used0_ref, used1_ref, dk_ref, dv_ref, sk_ref, sv_ref, dq_ref, kt_ref):
    h = pl.program_id(0)
    masks = head_masks()
    for c in range(2):
        lanes = slice(c * BLK, (c + 1) * BLK)
        for r in range(4):
            kt_ref[r, :, lanes] = flip(k_ref[r, c])
        kt_ref[4, :, lanes] = flip(ks_ref[0, c])
    for ref in (dk_ref, dv_ref, sk_ref, sv_ref):
        ref[...] = jnp.zeros_like(ref)

    def one(row, key_rows):
        tasks = []
        for c, delta_ref, used_ref in ((0, delta0_ref, used0_ref), (1, delta1_ref, used1_ref)):
            lse = [lse_ref[row, c, pl.ds(2 * h + i, 1), :] for i in range(2)]
            delta = [delta_ref[row, pl.ds(2 * h + i, 1), :] for i in range(2)]
            keys, values, keys_t, biases = [], [], [], []
            for r in key_rows:
                for kc in range(2):
                    sibling = r in (-1, 4)
                    keys.append(ks_ref[0, kc] if sibling else k_ref[r, kc])
                    values.append(ks_ref[1, kc] if sibling else v_ref[r, kc])
                    keys_t.append(kt_ref[4 if sibling else r, :, kc * BLK : (kc + 1) * BLK])
                    at = offset_row(r - row, kc - c)
                    biases.append(twice((1.0 - used_ref[row, at : at + 1, :]) * FAR))
            query = (q_ref[row, c], do_ref[row, c], cat(lse, 1), cat(delta, 1), biases)
            tasks.append((query, keys, values, keys_t))
        results = attend(tasks, masks)
        dk = results[0][0] + results[1][0]
        dv = results[0][1] + results[1][1]
        for n, r in enumerate(key_rows):
            for kc in range(2):
                part = slice((2 * n + kc) * BLK, (2 * n + kc + 1) * BLK)
                if r in (-1, 4):
                    sk_ref[kc] += dk[part]
                    sv_ref[kc] += dv[part]
                else:
                    dk_ref[r, kc] += dk[part]
                    dv_ref[r, kc] += dv[part]
        for c in range(2):
            dq_ref[row, c] = results[c][2].T * SCALE

    def run(groups):
        for row, key_rows in groups:
            one(row, key_rows)

    by_rows(pos_ref[0], run)


def received(ref, at, lanes, aux, rows):
    lse = aux[0:2] + aux[2:4]
    delta = aux[4:6] + aux[6:8]
    biases = [twice((1.0 - row) * FAR) for row in rows]
    stats = [cat([x[0:1], x[1:2]], 1) for x in (lse, delta)]
    return (ref[at, 0:BLK, lanes], ref[at, BLK : 2 * BLK, lanes], stats[0], stats[1], biases)


def column_kernel(pos_ref, k_ref, v_ref, ks_ref, col_ref, dkp_ref, dvp_ref, skp_ref, svp_ref, *rest, side, sub):
    dk_ref, dv_ref, sib_ref, tail_ref, res_ref, kt_ref, acck_ref, accv_ref, accs_ref = rest[-9:]
    masks = head_masks()
    for n in range(sub):
        lanes = slice(n * PAIR, (n + 1) * PAIR)
        for r in range(4):
            kt_ref[n, :, r * BLK : (r + 1) * BLK] = flip(k_ref[r, 0, :, lanes])
        kt_ref[n, :, 4 * BLK :] = flip(ks_ref[0, 0, :, lanes])
    acck_ref[...] = dkp_ref[:, 0]
    accv_ref[...] = dvp_ref[:, 0]
    accs_ref[0] = skp_ref[0]
    accs_ref[1] = svp_ref[0]

    def run(groups):
        tasks, places = [], []
        for n in range(sub):
            lanes = slice(n * PAIR, (n + 1) * PAIR)
            for row, key_rows in groups:
                aux = col_ref[row, 2 * BLK : PAY, lanes].astype(jnp.float32)
                keys, values, keys_t, rows = [], [], [], []
                for r in key_rows:
                    sibling = r in (-1, 4)
                    keys.append(ks_ref[0, 0, :, lanes] if sibling else k_ref[r, 0, :, lanes])
                    values.append(ks_ref[1, 0, :, lanes] if sibling else v_ref[r, 0, :, lanes])
                    at = 4 * BLK if sibling else r * BLK
                    keys_t.append(kt_ref[n, :, at : at + BLK])
                    at = 8 + offset_row(r - row, 1 - 2 * side)
                    rows.append(aux[at : at + 1])
                tasks.append((received(col_ref, row, lanes, aux, rows), keys, values, keys_t))
                places.append((row, key_rows, lanes))
        for (row, key_rows, lanes), (dk, dv, dq_t) in zip(places, attend(tasks, masks)):
            for n, r in enumerate(key_rows):
                part = slice(n * BLK, (n + 1) * BLK)
                if r in (-1, 4):
                    accs_ref[0, :, lanes] += dk[part]
                    accs_ref[1, :, lanes] += dv[part]
                else:
                    acck_ref[r, :, lanes] += dk[part]
                    accv_ref[r, :, lanes] += dv[part]
            res_ref[row, :, lanes] = (dq_t.T * SCALE).astype(jnp.bfloat16)

    by_rows(pos_ref[0], run, together=True)
    for r in range(4):
        dk_ref[r, 0] = acck_ref[r].astype(jnp.bfloat16)
        dv_ref[r, 0] = accv_ref[r].astype(jnp.bfloat16)
    sib_ref[0] = accs_ref[...].astype(jnp.bfloat16)
    for i in range(2):
        tail_ref[i, 0, 0] = acck_ref[3 * i]
        tail_ref[i, 0, 1] = accv_ref[3 * i]


def outer_kernel(pos_ref, k_ref, v_ref, out_ref, dg0_ref, dg1_ref, part_ref, ro_ref, rg0_ref, rg1_ref):
    masks = head_masks()
    below = pos_ref[0] == 0
    slots = ((dg0_ref, 0, rg0_ref, -1), (out_ref, 0, ro_ref, 0), (out_ref, 1, ro_ref, 1), (dg1_ref, 0, rg1_ref, 2))
    tasks, places = [], []
    for n in range(SUB):
        lanes = slice(n * PAIR, (n + 1) * PAIR)
        kts = [flip(k_ref[0, c, :, lanes]) for c in range(2)]
        for ref, at, res_ref, c in slots:
            near = [kc for kc in range(2) if abs(kc - c) <= 1]
            aux = ref[at, 2 * BLK : PAY, lanes].astype(jnp.float32)
            ups = [8 + kc - c + 1 for kc in near]
            rows = [jnp.where(below, aux[u + 5 : u + 6], aux[u : u + 1]) for u in ups]
            query = received(ref, at, lanes, aux, rows)
            keys = [k_ref[0, kc, :, lanes] for kc in near]
            values = [v_ref[0, kc, :, lanes] for kc in near]
            tasks.append((query, keys, values, [kts[kc] for kc in near]))
            places.append((lanes, at, res_ref, near))
    totals = {}
    for (lanes, at, res_ref, near), (dk, dv, dq_t) in zip(places, attend(tasks, masks)):
        for n, kc in enumerate(near):
            for i, x in enumerate((dk, dv)):
                x = x[n * BLK : (n + 1) * BLK]
                key = (kc, i, lanes.start)
                totals[key] = totals[key] + x if key in totals else x
        res_ref[at, :, lanes] = (dq_t.T * SCALE).astype(jnp.bfloat16)
    for (kc, i, start), x in totals.items():
        part_ref[kc, i, :, start : start + PAIR] = x


def queries_kernel(pos_ref, dq_ref, back_ref, row_ref, corner_ref, *rest):
    res_ref = rest[-1]
    for r in range(2):
        total = dq_ref[r, 0] + back_ref[r].astype(jnp.float32)
        edge = row_ref[0].astype(jnp.float32) + corner_ref[0].astype(jnp.float32)
        outer = 2 * pl.program_id(0) + r == 3 * pos_ref[0]
        res_ref[r, 0] = jnp.where(outer, total + edge, total).astype(jnp.bfloat16)


def edges_kernel(pos_ref, tail_ref, part_ref, sib_ref, dk_in, dv_in, dk_ref, dv_ref):
    outer = pl.program_id(0) == pos_ref[0]
    for c in range(2):
        for i, ref in enumerate((dk_ref, dv_ref)):
            add = jnp.where(outer, part_ref[c, i], sib_ref[c, i].astype(jnp.float32))
            ref[0, c] = (tail_ref[0, c, i] + add).astype(jnp.bfloat16)


def lanes_spec(shape, base=0, at=None):
    at = at or (0,) * (len(shape) - 1)
    return pl.BlockSpec(shape, lambda h, *_: at + (h + base,))


def rows_spec(shape, lane=0):
    return pl.BlockSpec(shape, lambda r, *_: (r,) + (0,) * (len(shape) - 2) + (lane,))


def fixed(shape, lane=0):
    return pl.BlockSpec(shape, lambda *_: (0,) * (len(shape) - 1) + (lane,))


SMEM = pl.BlockSpec(memory_space=pltpu.SMEM)
ANY = pl.BlockSpec(memory_space=pl.ANY)
TILES = (4, 2, BLK, PAIR)
FULL = PAIRS * PAIR


def sds(shape, dtype=jnp.bfloat16):
    return jax.ShapeDtypeStruct(shape, dtype)


def f32s(shape):
    return sds(shape, jnp.float32)


def call(kernel, name, grid, ins, outs, shapes, scratch=(), alias=None):
    return pl.pallas_call(
        kernel,
        grid_spec=pltpu.PrefetchScalarGridSpec(
            num_scalar_prefetch=1, grid=(grid,), in_specs=ins, out_specs=outs, scratch_shapes=scratch
        ),
        out_shape=shapes,
        input_output_aliases=alias or {},
        compiler_params=pltpu.CompilerParams(
            vmem_limit_bytes=VMEM, dimension_semantics=("arbitrary",)
        ),
        cost_estimate=pl.CostEstimate(flops=1, bytes_accessed=1, transcendentals=0),
        name=name,
    )


def prepare_column(pos, lists, q, do, o, lse, c, parts):
    block = pl.BlockSpec((1, 1, BLK, FULL), lambda r, _: (r, c, 0, 0))
    shapes = [(2 * PAIRS, BLK), (16, BLK)] + [(PAY, n * PAIR) for n in parts]
    kinds = [jnp.float32, jnp.float32] + [jnp.bfloat16] * len(parts)
    return call(
        functools.partial(prepare_column_kernel, c=c),
        "prepare_column",
        4,
        [SMEM] * 2 + [block] * 3 + [rows_spec((1, 2, 2 * PAIRS, BLK))],
        [rows_spec((1,) + shape) for shape in shapes],
        [sds((4,) + shape, kind) for shape, kind in zip(shapes, kinds)],
        [pltpu.VMEM((16, FULL), jnp.float32)],
    )(pos, *lists, q, do, o, lse)


def prepare_row(pos, lists, q, do, o, lse):
    outer = lambda shape: pl.BlockSpec(shape, lambda _, p: (3 * p[0], 0, 0, 0))
    shapes = [(2, PAY, FULL), (1, PAY, FULL), (1, PAY, FULL)]
    return call(
        prepare_row_kernel,
        "prepare_row",
        1,
        [SMEM] * 2 + [outer((1, 2, BLK, FULL))] * 3 + [outer((1, 2, 2 * PAIRS, BLK))],
        [fixed(shape) for shape in shapes],
        [sds(shape) for shape in shapes],
        [pltpu.VMEM((2, 16, BLK), jnp.float32), pltpu.VMEM((2, 16, FULL), jnp.float32)],
    )(pos, *lists, q, do, o, lse)


def local(pos, q, do, k, v, ks, lse, deltas, used):
    tiles = f32s((4, 2, BLK, FULL))
    edge = f32s((2, BLK, FULL))
    return call(
        local_kernel,
        "local",
        PAIRS,
        [lanes_spec(TILES)] * 4
        + [lanes_spec((2, 2, BLK, PAIR)), fixed((4, 2, 2 * PAIRS, BLK))]
        + [fixed((4, 2 * PAIRS, BLK))] * 2
        + [fixed((4, 16, BLK))] * 2,
        [lanes_spec(TILES)] * 2 + [lanes_spec((2, BLK, PAIR))] * 2 + [lanes_spec(TILES)],
        [tiles, tiles, edge, edge, tiles],
        [pltpu.VMEM((5, PAIR, 2 * BLK), jnp.bfloat16)],
    )(pos, q, do, k, v, ks, lse, *deltas, *used)


def column(pos, k, v, ks, col, parts, done, base, count, side):
    sub = SUB if count % SUB == 0 else 1
    wide = sub * PAIR
    at = base // sub
    column_of = lanes_spec((4, 1, BLK, wide), at, (0, side, 0))
    return call(
        functools.partial(column_kernel, side=side, sub=sub),
        "column",
        count // sub,
        [column_of] * 2
        + [lanes_spec((2, 1, BLK, wide), at, (0, side, 0)), lanes_spec((4, PAY, wide))]
        + [column_of] * 2
        + [lanes_spec((1, BLK, wide), at, (side, 0))] * 2
        + [ANY] * len(done),
        [column_of] * 2
        + [
            lanes_spec((1, 2, BLK, wide), at, (side, 0, 0)),
            lanes_spec((2, 1, 2, BLK, wide), at, (0, side, 0, 0)),
            lanes_spec((4, BLK, wide)),
        ],
        [sds((4, 2, BLK, FULL))] * 2
        + [sds((2, 2, BLK, FULL)), f32s((2, 2, 2, BLK, FULL)), sds((4, BLK, count * PAIR))],
        [pltpu.VMEM((sub, PAIR, 5 * BLK), jnp.bfloat16)]
        + [pltpu.VMEM((4, BLK, wide), jnp.float32)] * 2
        + [pltpu.VMEM((2, BLK, wide), jnp.float32)],
        alias={9 + i: i for i in range(len(done))},
    )(pos, k, v, ks, col, *parts, *done)


def outers(pos, k, v, out, dg0, dg1):
    sizes = (2, 1, 1)
    wide = SUB * PAIR
    outer = pl.BlockSpec((1, 2, BLK, wide), lambda h, p: (3 * p[0], 0, 0, h))
    return call(
        outer_kernel,
        "outer_rows",
        PAIRS // SUB,
        [outer] * 2 + [lanes_spec((n, PAY, wide)) for n in sizes],
        [lanes_spec((2, 2, BLK, wide))] + [lanes_spec((n, BLK, wide)) for n in sizes],
        [f32s((2, 2, BLK, FULL))] + [sds((n, BLK, FULL)) for n in sizes],
    )(pos, k, v, out, dg0, dg1)


def finish_queries(pos, dqp, back, back_out, corner, done, c, base, count):
    wide = count * PAIR
    lane = base // count
    block = pl.BlockSpec((2, 1, BLK, wide), lambda r, *_: (r, c, 0, lane))
    edge = lambda at: pl.BlockSpec((1, BLK, wide), lambda *_: (at, 0, lane))
    return call(
        queries_kernel,
        "finish_queries",
        2,
        [block, rows_spec((2, BLK, wide)), edge(c), edge(0)] + [ANY] * len(done),
        block,
        sds((4, 2, BLK, FULL)),
        alias={5 + i: i for i in range(len(done))},
    )(pos, dqp, back, back_out, corner, *done)


def finish_edges(pos, tail, part, sib, dk, dv):
    row = pl.BlockSpec((1, 2, BLK, FULL), lambda i, p: (3 * i, 0, 0, 0))
    edge = (2, 2, BLK, FULL)
    return call(
        edges_kernel,
        "finish_edges",
        2,
        [rows_spec((1,) + edge)] + [fixed(edge)] * 2 + [ANY] * 2,
        [row] * 2,
        [sds((4, 2, BLK, FULL))] * 2,
        alias={4: 0, 5: 1},
    )(pos, tail, part, sib, dk, dv)


def pairs_of(rows, cols):
    at = lambda s, p: (s % rows) * cols + p
    outer = lambda s: s + 1 if s % 2 else s - 1
    inner = lambda s: s - 1 if s % 2 else s + 1
    cells = [(s, p) for s in range(rows) for p in range(cols)]
    return {
        "right": [(at(s, p), at(s, p + 1)) for s, p in cells if p + 1 < cols],
        "left": [(at(s, p), at(s, p - 1)) for s, p in cells if p > 0],
        "outer": [(at(s, p), at(outer(s), p)) for s, p in cells],
        "inner": [(at(s, p), at(inner(s), p)) for s, p in cells],
        "outer_right": [(at(s, p), at(outer(s), p + 1)) for s, p in cells if p + 1 < cols],
        "outer_left": [(at(s, p), at(outer(s), p - 1)) for s, p in cells if p > 0],
    }


def after(pos, *others):
    return lax.optimization_barrier((pos,) + others)[0]


def on_device(rows, cols, q, k, v, o, do, lse, neighbours, flags):
    pairs = pairs_of(rows, cols)
    send = lambda x, way: lax.ppermute(x, AXES, pairs[way])
    row = lax.axis_index("slit")
    pos = jnp.stack([row % 2, row * 4, lax.axis_index("span") * 2]).astype(jnp.int32)
    lists = (neighbours, flags)

    out, dg0, dg1 = prepare_row(pos, lists, q, do, o, lse)
    halo_out = send(out, "outer")
    pos = after(pos, out)
    inner = 3 - 3 * (row % 2)
    kv = jnp.concatenate([lax.dynamic_slice_in_dim(x, inner, 1, 0) for x in (k, v)], axis=0)
    ks = send(kv, "inner")
    delta1, used1, col1 = prepare_column(pos, lists, q, do, o, lse, 1, [PAIRS])
    pos = after(pos, delta1)
    delta0, used0, *col0 = prepare_column(pos, lists, q, do, o, lse, 0, [FIRST, PAIRS - FIRST])
    from_left = send(after(col1, ks), "right")
    halo_g0 = send(dg1, "outer_right")
    halo_g1 = send(dg0, "outer_left")
    ready = (halo_out, ks, halo_g0, halo_g1)
    from_right = [send(after(x, *(ready if n else ready[:2])), "left") for n, x in enumerate(col0)]
    pos = after(pos, delta0)

    *parts, dqp = local(pos, q, do, k, v, ks, lse, (delta0, delta1), (used0, used1))
    pos = after(pos, dqp)
    part_out, ro, rg0, rg1 = outers(pos, k, v, halo_out, halo_g0, halo_g1)
    back_out = send(ro, "outer")
    back_g1 = send(rg0, "outer_left")
    back_g0 = send(rg1, "outer_right")
    pos = after(pos, ro)
    *done, res0 = column(pos, k, v, ks, from_left, parts, (), 0, PAIRS, 0)
    back1 = send(res0, "left")
    pos = after(pos, res0)
    *done, res1 = column(pos, k, v, ks, from_right[0], parts, done, 0, FIRST, 1)
    back0 = send(res1, "right")
    pos = after(pos, res1, back_out, back_g0, back_g1)
    dk, dv, sib, tail, res2 = column(pos, k, v, ks, from_right[1], parts, done, FIRST, PAIRS - FIRST, 1)
    back0_last = send(after(res2, back1), "right")

    dq = finish_queries(pos, dqp, back1, back_out, back_g1, (), 1, 0, PAIRS)
    back_sib = send(sib, "inner")
    pos = after(pos, dq)
    dk, dv = finish_edges(pos, tail, part_out, back_sib, dk, dv)
    pos = after(pos, dk)
    dq = finish_queries(pos, dqp, back0, back_out, back_g0, (dq,), 0, 0, FIRST)
    dq = finish_queries(pos, dqp, back0_last, back_out, back_g0, (dq,), 0, FIRST, PAIRS - FIRST)
    return dq, dk, dv


def solution(mesh):
    tile = P("slit", "span", None, None)
    row = P("slit", "span", None)
    body = functools.partial(on_device, mesh.shape["slit"], mesh.shape["span"])
    return jax.shard_map(
        body,
        mesh=mesh,
        in_specs=(tile,) * 6 + (row,) * 2,
        out_specs=(tile,) * 3,
        check_vma=False,
    )
```
